32 devices in a mesh: doc: 4 (over y, x), seq: 8 (over z, core).
Axes of the slice: x: 2, y: 2, z: 4, core: 2. Of those that a mesh axis runs over, the one named last changes fastest.
Arguments:
- hidden_in: bfloat16 [4, 4096, 2048], P('doc', 'seq'), may hold values from -6 to 6
- cotangent: bfloat16 [4, 4096, 2048], P('doc', 'seq'), may hold values from -6 to 6
- scan_init: float32 [4, 16, 4096], P('doc'), may hold values from -4 to 4
- conv_init: bfloat16 [4, 3, 4096], P('doc'), may hold values from -6 to 6
- norm_gain: bfloat16 [2048], P('seq'), may hold values from 0.5 to 1.5
- in_weight: bfloat16 [2048, 8192], P('seq'), may hold values from -0.125 to 0.125
- conv_weight: bfloat16 [4, 4096], P(None, 'seq'), may hold values from -3 to 3
- conv_bias: bfloat16 [4096], P('seq'), may hold values from -1.5 to 1.5
- xproj_weight: bfloat16 [4096, 160], P('seq'), may hold values from -0.09375 to 0.09375
- dt_weight: bfloat16 [128, 4096], P(None, 'seq'), may hold values from -0.5 to 0.5
- dt_bias: bfloat16 [4096], P('seq'), may hold values from -3.5 to -2.5
- a_log: bfloat16 [16, 4096], P(None, 'seq'), may hold values from -8.7 to 2.1
- skip_d: bfloat16 [4096], P('seq'), may hold values from 0.5 to 1.5
- out_weight: bfloat16 [2048, 4096], P('seq'), may hold values from -0.1875 to 0.1875
Outputs:
- output: bfloat16 [4, 4096, 2048], P('doc', 'seq')
- input_grad: float32 [4, 4096, 2048], P('doc', 'seq')
- scan_init_grad: float32 [4, 16, 4096], P('doc')
- conv_init_grad: float32 [4, 3, 4096], P('doc')
- norm_gain_grad: float32 [2048], P('seq')
- in_weight_grad: float32 [2048, 8192], P('seq')
- conv_weight_grad: float32 [4, 4096], P(None, 'seq')
- conv_bias_grad: float32 [4096], P('seq')
- xproj_weight_grad: float32 [4096, 160], P('seq')
- dt_weight_grad: float32 [128, 4096], P(None, 'seq')
- dt_bias_grad: float32 [4096], P('seq')
- a_log_grad: float32 [16, 4096], P(None, 'seq')
- skip_d_grad: float32 [4096], P('seq')
- out_weight_grad: float32 [2048, 4096], P('seq')
The draws below stay inside these ranges and needn't reach their ends.
All inputs are finite; a program needn't handle non-finite values.
Results may differ from the reference program's by a relative error of at most 0.014.
Values may be sent and summed in bfloat16 or wider, within the bound.
No kernel may reach another device: no remote copies, remote signals or barrier semaphores. Data moves between devices by JAX's collectives and lax.ppermute only.
A program may use at most 448 MiB of HBM per device.

```python
import math
import jax
import jax.numpy as jnp
from jax import lax

D = 2048
DI = 4096
N = 16
R = 128
KCONV = 4
SCAN_BLOCK = 32
LENGTH = 4096
DOCS = 4


def draw_a_log(key, part):
    key = jax.random.fold_in(key, 11)
    pick_key, slow_key, fast_key = jax.random.split(key, 3)
    share = 0.5
    slow_mask = jax.random.bernoulli(pick_key, share, (N, DI))
    slow_rate = jnp.exp(jax.random.uniform(slow_key, (N, DI), jnp.float32, math.log(0.3), math.log(2.0))) / (0.05 * LENGTH)
    fast_rate = jnp.exp(jax.random.uniform(fast_key, (N, DI), jnp.float32, math.log(0.3), math.log(8.0)))
    return jnp.log(jnp.where(slow_mask, slow_rate, fast_rate)).astype(jnp.bfloat16)


def with_spikes(array, rng, source, target, parts, factor):
    owner, partner = [(jnp.arange(array.shape[dim]) // (array.shape[dim] // parts)).reshape([-1 if axis == dim else 1 for axis in range(array.ndim)]) for dim in (source, target)]
    chosen = jax.random.permutation(rng, parts)[partner]
    strong = (owner == chosen) | (owner == (partner + parts // 2) % parts)
    return jnp.where(strong, factor * array, array)


def shard_levels(rng, shape, pieces, smallest, high):
    level, own = 1.0, jax.random.fold_in(rng, 6)
    for axis_at, parts in pieces:
        heights = jnp.exp(jax.random.uniform(jax.random.fold_in(own, axis_at), (parts,), jnp.float32, smallest / len(pieces), high / len(pieces)))
        level = level * jnp.repeat(heights, shape[axis_at] // parts).reshape([-1 if axis == axis_at else 1 for axis in range(len(shape))])
    return level


def bell_draw(rng, extent, scale, most, cuts=(), kind=jnp.bfloat16):
    drawn = scale * jax.random.normal(rng, extent, jnp.float32)
    if cuts:
        drawn = drawn * shard_levels(rng, extent, cuts, -0.22, 0.18)
    return jnp.clip(drawn, -most, most).astype(kind)


def bell_draw_with(stream_key, shape, scale, reach, cuts, heavy, held_as=jnp.bfloat16):
    values = scale * jax.random.normal(stream_key, shape, jnp.float32)
    if cuts:
        values = values * shard_levels(stream_key, shape, cuts, -0.22, 0.18)
    return jnp.clip(with_spikes(values, jax.random.fold_in(stream_key, 3), *heavy), -reach, reach).astype(held_as)


def setup_inputs(seed: int = 0) -> dict:
    arg_keys = jax.random.split(jax.random.key(seed), 15)
    return {
        "hidden_in": bell_draw_with(arg_keys[0], (DOCS, LENGTH, D), 1.0, 6.0, ((0, 4), (1, 8)), (1, 2, 8, 2.0)),
        "cotangent": bell_draw_with(arg_keys[1], (DOCS, LENGTH, D), 1.0, 6.0, ((0, 4), (1, 8)), (1, 2, 8, 2.0)),
        "scan_init": bell_draw(arg_keys[2], (DOCS, N, DI), 0.5, 4.0, ((0, 4),), jnp.float32),
        "conv_init": bell_draw(arg_keys[3], (DOCS, KCONV - 1, DI), 1.0, 6.0, ((0, 4),)),
        "norm_gain": jnp.clip(1.0 + 0.1 * jax.random.normal(arg_keys[4], (D,), jnp.float32), 0.5, 1.5).astype(jnp.bfloat16),
        "in_weight": bell_draw(arg_keys[5], (D, 2 * DI), D ** -0.5, 0.125, ((0, 8),)),
        "conv_weight": bell_draw(arg_keys[6], (KCONV, DI), KCONV ** -0.5, 3.0, ((1, 8),)),
        "conv_bias": bell_draw(arg_keys[7], (DI,), 0.3, 1.5, ((0, 8),)),
        "xproj_weight": bell_draw(arg_keys[8], (DI, R + 2 * N), DI ** -0.5, 0.09375, ((0, 8),)),
        "dt_weight": bell_draw(arg_keys[9], (R, DI), R ** -0.5, 0.5, ((1, 8),)),
        "dt_bias": jnp.clip(-3.5 + 1.0 * jax.random.uniform(arg_keys[10], (DI,), jnp.float32) ** shard_levels(arg_keys[10], (DI,), ((0, 8),), -0.2, 0.2), -3.5, -2.5).astype(jnp.bfloat16),
        "a_log": draw_a_log(jax.random.fold_in(arg_keys[14], 71), 0),
        "skip_d": jnp.clip(0.5 + 1.0 * jax.random.uniform(arg_keys[12], (DI,), jnp.float32) ** shard_levels(arg_keys[12], (DI,), ((0, 8),), -0.2, 0.2), 0.5, 1.5).astype(jnp.bfloat16),
        "out_weight": bell_draw(arg_keys[13], (D, DI), (DI // 4) ** -0.5, 0.1875, ((0, 8),)),
    }


NORM_EPS = 1e-05

@jax.custom_vjp
def low(v):
    return lax.optimization_barrier(v.astype(jnp.bfloat16)).astype(jnp.float32)

@jax.custom_vjp
def low_back(v):
    return v

def low_keep(v):
    return (low(v), None)

def low_pass(kept, grad):
    return (grad,)

def back_keep(v):
    return (v, None)

def back_low(kept, grad):
    return (low(grad),)
low.defvjp(low_keep, low_pass)
low_back.defvjp(back_keep, back_low)

def exact_dot(left, right):
    return jnp.dot(left, right, precision=lax.Precision.HIGHEST, preferred_element_type=jnp.float32)

def scan_block(state_now, blk_rows, neg_rate):
    outputs = []
    for position in range(blk_rows[0].shape[0]):
        decay_now = jnp.exp(blk_rows[0][position][None, :] * neg_rate)
        state_now = decay_now * state_now + blk_rows[2][position][:, None] * blk_rows[1][position][None, :]
        if len(blk_rows) == 4:
            outputs.append(lax.optimization_barrier(jnp.sum(blk_rows[3][position][:, None] * state_now, axis=0)))
    if len(blk_rows) == 4:
        return (state_now, jnp.stack(outputs))
    return (state_now, None)

def run_blocks(state_now, inputs, neg_rate):
    blocks = inputs[0].shape[0] // SCAN_BLOCK
    blocked = tuple((value.reshape((blocks, SCAN_BLOCK) + value.shape[1:]) for value in inputs))

    def block_step(carry_in, blk_rows):
        return scan_block(carry_in, blk_rows, neg_rate)
    final_state, outputs = lax.scan(jax.checkpoint(block_step), state_now, blocked)
    if outputs is None:
        return (final_state, None)
    return (final_state, outputs.reshape(inputs[0].shape))

def mamba_layer(residual, start_state, conv_state, norm_gain, in_weight, conv_weight, conv_bias, xproj_weight, dt_weight, dt_bias, a_log, skip_d, out_weight):
    tokens = residual.shape[0]
    inv_scale = lax.rsqrt(lax.optimization_barrier(jnp.mean(residual * residual, axis=1, keepdims=True)) + NORM_EPS)
    normed = low(residual * inv_scale * norm_gain)
    projected = low_back(exact_dot(normed, in_weight))
    inner_x = projected[:, :DI]
    gate_in = projected[:, DI:]
    extended = jnp.concatenate([conv_state, inner_x], axis=0)
    conv_pre = conv_bias + conv_weight[0] * extended[:tokens]
    for offset in range(1, KCONV):
        conv_pre = conv_pre + conv_weight[offset] * extended[offset:offset + tokens]
    mixed = low(jax.nn.silu(conv_pre))
    xdbl_rows = low_back(exact_dot(mixed, xproj_weight))
    rank_in = low(xdbl_rows[:, :R])
    b_rows = xdbl_rows[:, R:R + N]
    c_rows = xdbl_rows[:, R + N:]
    step_size = jax.nn.softplus(low_back(exact_dot(rank_in, dt_weight)) + dt_bias)
    neg_rate = -jnp.exp(a_log)
    scanned = run_blocks(start_state, (step_size, step_size * mixed, b_rows, c_rows), neg_rate)[1]
    y_total = scanned + skip_d * mixed
    gated_out = low(y_total * jax.nn.silu(gate_in))
    return residual + exact_dot(gated_out, out_weight.T)

def reference(hidden_in, cotangent, scan_init, conv_init, norm_gain, in_weight, conv_weight, conv_bias, xproj_weight, dt_weight, dt_bias, a_log, skip_d, out_weight):
    params = tuple((weight.astype(jnp.float32) for weight in (norm_gain, in_weight, conv_weight, conv_bias, xproj_weight, dt_weight, dt_bias, a_log, skip_d, out_weight)))

    def one_doc(totals, doc_rows):
        residual, cot_rows, start_state, conv_state = doc_rows
        result, pullback = jax.vjp(mamba_layer, residual.astype(jnp.float32), start_state, conv_state.astype(jnp.float32), *params)
        grads = pullback(cot_rows.astype(jnp.float32))
        totals = tuple((running + fresh for running, fresh in zip(totals, grads[3:])))
        return (totals, (result.astype(jnp.bfloat16), grads[0], grads[1], grads[2]))
    zero_grads = tuple((jnp.zeros(weight.shape, jnp.float32) for weight in params))
    totals, per_doc = lax.scan(one_doc, zero_grads, (hidden_in, cotangent, scan_init, conv_init))
    return (per_doc[0], per_doc[1], per_doc[2], per_doc[3], totals[0], totals[1], totals[2], totals[3], totals[4], totals[5], totals[6], totals[7], totals[8], totals[9])
```

```python
import functools
import jax
import jax.numpy as jnp
from jax import lax
from jax.experimental import pallas as pl
from jax.experimental.pallas import tpu as pltpu
from jax.sharding import PartitionSpec as P

TB = 16
F32 = jnp.float32
BF = jnp.bfloat16
LN2 = 0.6931471805599453
NORM_EPS = 1e-05
LAST = (((1,), (1,)), ((), ()))
FIRST = (((0,), (0,)), ((), ()))


def mm(a, b):
    return jnp.dot(a, b, preferred_element_type=F32)


def mm_last(a, b):
    return lax.dot_general(a, b, LAST, preferred_element_type=F32)


def mm_first(a, b):
    return lax.dot_general(a, b, FIRST, preferred_element_type=F32)


def cost(us):
    return pl.CostEstimate(flops=int(us * 1.0e9), bytes_accessed=0, transcendentals=0)


def params():
    return pltpu.CompilerParams(vmem_limit_bytes=56 * 2**20)


def shape(dims, kind=F32):
    return jax.ShapeDtypeStruct(dims, kind)


def whole(dims):
    return pl.BlockSpec(dims, lambda *_: (0,) * len(dims))


def tie(x, *tokens):
    free = pl.BlockSpec(memory_space=pl.ANY)
    return pl.pallas_call(lambda *refs: None, out_shape=shape(x.shape, x.dtype),
                          in_specs=[free] * (1 + len(tokens)), out_specs=free, input_output_aliases={0: 0},
                          name="tie")(x, *tokens)


def sigmoid(x):
    return 0.5 + 0.5 * jnp.tanh(0.5 * x)


def tiles(x):
    return sum(x[:, c:c + 128] for c in range(0, x.shape[1], 128))


def softplus(x):
    return jnp.maximum(x, 0.0) + jnp.log1p(jnp.exp(-jnp.abs(x)))


def front_kernel(first_ref, top_ref, low_ref, halo_ref, w_ref, few_ref, xproj_ref, init_ref, *refs, lead):
    taps, shift = few_ref[:lead + 1].astype(F32), few_ref[lead + 1:lead + 2].astype(F32)
    normed_ref, inner_ref, mixed_ref, rim_ref, proj_ref, xs_ref = refs[-6:]
    step, width = top_ref.shape[0], xs_ref.shape[1]

    def normalise(x):
        r = x.astype(F32)
        scale = lax.rsqrt(jnp.mean(r * r, axis=1, keepdims=True) + NORM_EPS)
        return (r * scale).astype(BF)

    @pl.when(pl.program_id(0) == 0)
    def _():
        before = mm(normalise(halo_ref[...]), w_ref[...])[halo_ref.shape[0] - 8:]
        rim = jnp.where(first_ref[0] == 1, init_ref[...], before)
        rim_ref[0] = rim
        xs_ref[:8] = rim

    in_top = 2 * pl.program_id(0) < pl.num_programs(0)
    normed_ref[...] = normalise(jnp.where(in_top, top_ref[...], low_ref[...]))
    x = mm(normed_ref[...], w_ref[...])
    inner_ref[0] = x
    xs_ref[8:] = x
    for c in range(0, width, 256):
        cs = pl.ds(c, 256)
        pre = shift[:, c:c + 256]
        for tap in range(lead + 1):
            pre = pre + taps[tap:tap + 1, c:c + 256] * xs_ref[pl.ds(8 - lead + tap, step), cs]
        mixed_ref[0, :, cs] = (pre * sigmoid(pre)).astype(BF)
    proj_ref[...] = mm_last(mixed_ref[0], xproj_ref[...])
    xs_ref[:8] = xs_ref[step:step + 8]


def front(slot, docs, kept, first, top, low, halo, w, small, lead, cols, init, step=128):
    width, block = w.shape
    extra = 16
    tokens = 2 * top.shape[0]
    count = tokens // step
    rows = pl.BlockSpec((1, step, block), lambda k: (slot, k, 0))
    few = pl.BlockSpec((1, 8, block), lambda k: (slot, 0, 0))
    return pl.pallas_call(
        functools.partial(front_kernel, lead=lead),
        out_shape=[shape((docs * tokens, width), BF), shape((docs, tokens, block)), shape((docs, tokens, block), BF),
                   shape((docs, 8, block)), shape((tokens, cols))],
        grid=(count,),
        in_specs=[pl.BlockSpec(memory_space=pltpu.SMEM), pl.BlockSpec((step, width), lambda k: (jnp.minimum(k, count // 2 - 1), 0)),
                  pl.BlockSpec((step, width), lambda k: (jnp.maximum(k - count // 2, 0), 0)),
                  pl.BlockSpec((extra, width), lambda k: (0, 0)), whole(w.shape),
                  whole((16, block)), pl.BlockSpec((cols, block), lambda k: (1, 0)), whole((8, block))]
        + [pl.BlockSpec(memory_space=pl.ANY)] * len(kept),
        out_specs=[pl.BlockSpec((step, width), lambda k: (slot * count + k, 0)), rows, rows, few,
                   pl.BlockSpec((step, cols), lambda k: (k, 0))],
        scratch_shapes=[pltpu.VMEM((step + 8, block), F32)],
        input_output_aliases={8 + i: i for i in range(len(kept))},
        compiler_params=params(), cost_estimate=cost(0.1), name="front",
    )(first, top, low, halo, w, small, small, init, *kept)


def summary_kernel(rank_ref, dtw_ref, shift_ref, mixed_ref, bt_ref, rate_ref, *refs):
    pre_ref, delta_ref, end_ref, decay_ref = refs[-4:]
    tokens, width = mixed_ref.shape[1:]
    rate = rate_ref[...]
    count = tokens // TB

    def steps(i):
        rows = pl.ds(pl.multiple_of(i * TB, TB), TB)
        pre = mm(rank_ref[0, rows], dtw_ref[...]) + shift_ref[...]
        pre_ref[0, rows] = pre
        delta_ref[0, rows] = softplus(pre)

    steps(0)

    def body(i, carry):
        h, total = carry
        rows = pl.ds(pl.multiple_of(i * TB, TB), TB)
        dl = delta_ref[0, rows]
        dr = dl * mixed_ref[0, rows].astype(F32)
        bt = bt_ref[0, i]
        for t in range(TB):
            h = jnp.exp2(dl[t:t + 1] * rate) * h + bt[:, t:t + 1] * dr[t:t + 1]
        steps(jnp.minimum(i + 1, count - 1))
        return h, total + dl

    h, total = lax.fori_loop(0, count, body, (jnp.zeros(rate.shape, F32), jnp.zeros((TB, width), F32)))
    end_ref[0] = h
    decay_ref[0] = jnp.exp2(jnp.sum(total, axis=0, keepdims=True) * rate)


def chained(kept, before):
    return [pl.BlockSpec(memory_space=pl.ANY)] * len(kept), {before + i: i for i in range(len(kept))}


def summary(base, count, kept, rank_in, dtw, shift, mixed, bt, rate):
    docs, tokens, width = mixed.shape
    n, rank = rate.shape[0], rank_in.shape[2]
    rows = pl.BlockSpec((1, tokens, width), lambda g: (g + base, 0, 0))
    state = pl.BlockSpec((1, n, width), lambda g: (g, 0, 0))
    free, alias = chained(kept, 6)
    return pl.pallas_call(
        summary_kernel,
        out_shape=[shape((docs, tokens, width))] * 2 + [shape((count, n, width))] * 2,
        grid=(count,),
        in_specs=[pl.BlockSpec((1, tokens, rank), lambda g: (g + base, 0, 0)), whole(dtw.shape), whole((1, width)), rows,
                  pl.BlockSpec((1, tokens // TB, n, TB), lambda g: (g + base, 0, 0, 0)), whole(rate.shape)] + free,
        out_specs=[rows, rows, state, state], input_output_aliases=alias,
        compiler_params=params(), cost_estimate=cost(22), name="summary",
    )(rank_in, dtw, shift, mixed, bt, rate, *kept)


def forward_kernel(delta_ref, mixed_ref, gate_ref, dg_ref, bt_ref, cdiag_ref, rate_ref, start_ref, mask_ref, skip_ref,
                   *refs):
    dy_ref, before_ref, gated_ref, dgate_ref, dout_ref, dstart_ref, sgrad_ref, hs_ref, ps_ref, hb_ref, zb_ref, sb_ref = refs[-12:]
    tokens = delta_ref.shape[1]
    n = rate_ref.shape[0]
    count = tokens // TB
    rate = rate_ref[...]

    @pl.when(pl.program_id(1) == 0)
    def _():
        hs_ref[...] = start_ref[0]
        ps_ref[...] = jnp.ones_like(ps_ref)
        dstart_ref[0] = jnp.zeros(dstart_ref.shape[1:], F32)
        sgrad_ref[0] = jnp.zeros(sgrad_ref.shape[1:], F32)

    mask = mask_ref[...]
    spread = lax.rem(lax.broadcasted_iota(jnp.int32, mask.shape, 1), n) == lax.broadcasted_iota(jnp.int32, mask.shape, 0)

    def finish(i, hm, good):
        rows = pl.ds(pl.multiple_of(i * TB, TB), TB)
        gate, dg = gate_ref[0, rows], dg_ref[0, rows]
        sig = sigmoid(gate)
        act = gate * sig
        mx = mixed_ref[0, rows].astype(F32)
        dy = dg * act
        dy_ref[0, rows] = dy
        sgrad_ref[0] += jnp.where(good, dy * mx, 0.0)
        y = mm(cdiag_ref[0, i], hm) + skip_ref[...] * mx
        gated_ref[0, rows] = (y * act).astype(BF)
        dgate_ref[0, rows] = (dg * y * (sig * (1.0 + gate * (1.0 - sig)))).astype(BF)
        dout_ref[0, i] = mm_last(jnp.ones((8, 128), BF), sb_ref[...])[:1]
        weight = jnp.where(spread, jnp.sum(cdiag_ref[0, i].astype(F32), axis=0, keepdims=True), 0.0).astype(BF)
        dstart_ref[0] += jnp.where(good, mm(weight, zb_ref[...]), 0.0)

    def body(i, carry):
        h, p = carry
        rows = pl.ds(pl.multiple_of(i * TB, TB), TB)
        dl = delta_ref[0, rows]
        dr = dl * mixed_ref[0, rows].astype(F32)
        gate = gate_ref[0, rows]
        dy = dg_ref[0, rows] * gate * sigmoid(gate)
        bt = bt_ref[0, i]
        hb = h.astype(BF)
        before_ref[0, pl.ds(pl.multiple_of(i * TB * n, TB * n), n)] = hb
        last = jnp.maximum(i - 1, 0)
        finish(last, before_ref[0, pl.ds(pl.multiple_of((last * TB + 1) * n, n), TB * n)], i > 0)
        for t in range(TB):
            if t:
                before_ref[0, pl.ds(pl.multiple_of((i * TB + t) * n, n), n)] = hb
            a = jnp.exp2(dl[t:t + 1] * rate)
            h = a * h + bt[:, t:t + 1] * dr[t:t + 1]
            hb = h.astype(BF)
            sb_ref[t * n:(t + 1) * n] = tiles(h * dy[t:t + 1]).astype(BF)
            p = p * a
            zb_ref[t * n:(t + 1) * n] = (p * dy[t:t + 1]).astype(BF)
        return h, p

    h, p = lax.fori_loop(0, count, body, (hs_ref[...], ps_ref[...]))
    hs_ref[...] = h
    ps_ref[...] = p
    hb_ref[:(TB - 1) * n] = before_ref[0, ((count - 1) * TB + 1) * n:count * TB * n]
    hb_ref[(TB - 1) * n:] = h.astype(BF)
    finish(count - 1, hb_ref[...], True)


def forward(base, part, kept, delta, mixed, gate, d_gated, bt, cdiag, rate, start, mask, skip, step=128):
    docs, tokens, width = delta.shape
    n, nb = rate.shape[0], step // TB
    rows = pl.BlockSpec((1, step, width), lambda g, k: (g + base, k, 0))
    own = pl.BlockSpec((1, step, width), lambda g, k: (g, k, 0))
    state = pl.BlockSpec((1, n, width), lambda g, k: (g, 0, 0))
    cols = pl.BlockSpec((1, nb, n, TB), lambda g, k: (g + base, k, 0, 0))
    free, alias = chained(kept, 10)
    return pl.pallas_call(
        forward_kernel,
        out_shape=[shape(delta.shape), shape((docs, tokens * n, width), BF), shape(delta.shape, BF), shape(delta.shape, BF),
                   shape((docs, tokens // TB, 1, TB * n)), shape((part, n, width)), shape((part, TB, width))],
        grid=(part, tokens // step),
        in_specs=[rows, rows, rows, own, cols, pl.BlockSpec((1, nb, TB, TB * n), lambda g, k: (g + base, k, 0, 0)),
                  whole(rate.shape), state, whole(mask.shape), whole((1, width))] + free,
        out_specs=[rows, pl.BlockSpec((1, step * n, width), lambda g, k: (g + base, k, 0)), rows, rows,
                   pl.BlockSpec((1, nb, 1, TB * n), lambda g, k: (g + base, k, 0, 0)), state,
                   pl.BlockSpec((1, TB, width), lambda g, k: (g, 0, 0))],
        scratch_shapes=[pltpu.VMEM((n, width), F32), pltpu.VMEM((n, width), F32), pltpu.VMEM((TB * n, width), BF),
                        pltpu.VMEM((TB * n, width), BF), pltpu.VMEM((TB * n, 128), BF)],
        input_output_aliases=alias, compiler_params=params(), cost_estimate=cost(45), name="forward",
    )(delta, mixed, gate, d_gated, bt, cdiag, rate, start, mask, skip, *kept)


def backward_kernel(pre_ref, delta_ref, mixed_ref, dy_ref, before_ref, ct_ref, bdiag_ref, rate_ref, qin_ref, mask_ref, skip_ref,
                    *refs):
    dpre_ref, dmix_ref, din_ref, drate_ref, bgrad_ref, qout_ref, ps_ref, qb_ref, wb_ref, sb_ref = refs[-10:]
    tokens = delta_ref.shape[1]
    n = rate_ref.shape[0]
    count = tokens // TB
    rate = rate_ref[...]

    @pl.when(pl.program_id(1) == 0)
    def _():
        ps_ref[...] = qin_ref[0]
        drate_ref[0] = jnp.zeros(drate_ref.shape[1:], F32)
        bgrad_ref[0] = jnp.zeros(bgrad_ref.shape[1:], F32)

    mask = mask_ref[...]
    spread = lax.rem(lax.broadcasted_iota(jnp.int32, mask.shape, 1), n) == lax.broadcasted_iota(jnp.int32, mask.shape, 0)
    sums = jnp.concatenate([mask, spread.astype(F32)], axis=0).astype(BF)

    fold = jnp.ones((8, 128), BF)

    def finish(i, good, side):
        rows = pl.ds(pl.multiple_of(i * TB, TB), TB)
        dl = delta_ref[0, rows]
        mx = mixed_ref[0, rows].astype(F32)
        d_drive = mm(bdiag_ref[0, i], qb_ref[side])
        both = LN2 * mm(sums, wb_ref[side])
        din_ref[0, i] = mm_last(fold, sb_ref[side])[:1]
        drate_ref[0] += jnp.where(good, both[TB:], 0.0)
        sig = sigmoid(pre_ref[0, rows])
        d_pre = both[:TB] * jnp.where(dl > 1e-30, sig / dl, 1.0) + mx * d_drive * sig
        dpre_ref[0, rows] = d_pre.astype(BF)
        bgrad_ref[0] += jnp.where(good, d_pre, 0.0)
        dmix_ref[0, rows] = dl * d_drive + dy_ref[0, rows] * skip_ref[...]

    def scan(i, p, side):
        rows = pl.ds(pl.multiple_of(i * TB, TB), TB)
        dl = delta_ref[0, rows]
        dr = dl * mixed_ref[0, rows].astype(F32)
        dy = dy_ref[0, rows]
        ct = ct_ref[0, i]
        for t in reversed(range(TB)):
            q = ct[:, t:t + 1] * dy[t:t + 1] + p
            qb_ref[side, t * n:(t + 1) * n] = q.astype(BF)
            sb_ref[side, t * n:(t + 1) * n] = tiles(q * dr[t:t + 1]).astype(BF)
            x = dl[t:t + 1] * rate
            p = jnp.exp2(x) * q
            e = p * before_ref[0, pl.ds(pl.multiple_of((i * TB + t) * n, n), n)].astype(F32)
            wb_ref[side, t * n:(t + 1) * n] = (x * e).astype(BF)
        return p

    def body(j, p):
        i = count - 1 - 2 * j
        finish(jnp.minimum(i + 1, count - 1), j > 0, 1)
        p = scan(i, p, 0)
        finish(i, True, 0)
        return scan(i - 1, p, 1)

    ps_ref[...] = lax.fori_loop(0, count // 2, body, ps_ref[...])
    finish(0, True, 1)
    qout_ref[0] = ps_ref[...]


def backward(base, part, begin, kept, pre, delta, mixed, dy, before, ct, bdiag, rate, qin, mask, skip, step=128):
    docs, tokens, width = delta.shape
    n, nb, last = rate.shape[0], step // TB, (begin + tokens // 2) // step - 1
    rows = pl.BlockSpec((1, step, width), lambda g, k: (g + base, last - k, 0))
    state = pl.BlockSpec((1, n, width), lambda g, k: (g, 0, 0))
    line = pl.BlockSpec((1, nb, 1, TB * n), lambda g, k: (g + base, last - k, 0, 0))
    free, alias = chained(kept, 11)
    return pl.pallas_call(
        backward_kernel,
        out_shape=[shape(delta.shape, BF), shape(delta.shape), shape((docs, tokens // TB, 1, TB * n)),
                   shape((part, n, width)), shape((part, TB, width)), shape((part, n, width))],
        grid=(part, tokens // 2 // step),
        in_specs=[rows, rows, rows, rows, pl.BlockSpec((1, step * n, width), lambda g, k: (g + base, last - k, 0)),
                  pl.BlockSpec((1, nb, n, TB), lambda g, k: (g + base, last - k, 0, 0)),
                  pl.BlockSpec((1, nb, TB, TB * n), lambda g, k: (g + base, last - k, 0, 0)),
                  whole(rate.shape), state, whole(mask.shape), whole((1, width))] + free,
        out_specs=[rows, rows, line, state, pl.BlockSpec((1, TB, width), lambda g, k: (g, 0, 0)), state],
        scratch_shapes=[pltpu.VMEM((n, width), F32), pltpu.VMEM((2, TB * n, width), BF), pltpu.VMEM((2, TB * n, width), BF),
                        pltpu.VMEM((2, TB * n, 128), BF)],
        input_output_aliases=alias, compiler_params=params(), cost_estimate=cost(4), name="backward",
    )(pre, delta, mixed, dy, before, ct, bdiag, rate, qin, mask, skip, *kept)


def conv_back_kernel(dproj_ref, xproj_ref, dmix_ref, inner_ref, prev_ref, rim_ref, taps_ref, shift_ref, carry_ref, *refs,
                     lead, first):
    dinner_ref, tail_ref, head_ref, sums_ref, dm_ref, xs_ref, ds_ref = refs[-7:]
    step, width = dmix_ref.shape[1:]
    k = pl.program_id(1)

    @pl.when(k == 0)
    def _():
        ds_ref[step:] = carry_ref[0]
        sums_ref[0] = jnp.zeros(sums_ref.shape[1:], F32)

    dm_ref[...] = mm(dproj_ref[0], xproj_ref[...])
    xs_ref[:8] = jnp.where(k == pl.num_programs(1) - 1, rim_ref[0], prev_ref[0]) if first else prev_ref[0]
    xs_ref[8:] = inner_ref[0]
    cw = 256

    def tile(x):
        return jnp.sum(x.reshape(step // 8, 8, cw), axis=0)

    for c in range(0, width, cw):
        cs = pl.ds(c, cw)
        pre = shift_ref[:, cs]
        for tap in range(lead + 1):
            pre = pre + taps_ref[tap:tap + 1, cs] * xs_ref[pl.ds(8 - lead + tap, step), cs]
        sig = sigmoid(pre)
        d_conv = (dmix_ref[0, :, cs] + dm_ref[:, cs]) * (sig * (1.0 + pre * (1.0 - sig)))
        ds_ref[:step, cs] = d_conv
        sums_ref[0, :8, cs] += tile(d_conv)
        for tap in range(lead + 1):
            sums_ref[0, 8 + 8 * tap:16 + 8 * tap, cs] += tile(d_conv * xs_ref[pl.ds(8 - lead + tap, step), cs])
        back = taps_ref[lead:lead + 1, cs] * d_conv
        for m in range(1, lead + 1):
            back = back + taps_ref[lead - m:lead - m + 1, cs] * ds_ref[pl.ds(m, step), cs]
        dinner_ref[0, :, cs] = back.astype(BF)

        @pl.when(k == 0)
        def _():
            tail_ref[0, :, cs] = back[step - 8:]

        head_ref[0, :, cs] = d_conv[:8]
        ds_ref[step:, cs] = d_conv[:8]


def conv_back(begin, kept, carry, d_proj, xproj_t, d_mix, inner_x, rim, taps, shift, step=128):
    docs, tokens, width = d_mix.shape
    half = tokens // 2
    last = (begin + half) // step - 1
    count = half // step
    lead = taps.shape[0] - 1
    cols = xproj_t.shape[0]
    rows = pl.BlockSpec((1, step, width), lambda g, k: (g, last - k, 0))
    few = pl.BlockSpec((1, 8, width), lambda g, k: (g, 0, 0))
    sums = 8 * (lead + 2)
    free, alias = chained(kept, 9)
    return pl.pallas_call(
        functools.partial(conv_back_kernel, lead=lead, first=begin == 0),
        out_shape=[shape(d_mix.shape, BF), shape((docs, 8, width)), shape((docs, 8, width)), shape((docs, sums, width))],
        grid=(docs, count),
        in_specs=[pl.BlockSpec((1, step, cols), lambda g, k: (g, count - 1 - k, 0)), whole(xproj_t.shape), rows, rows,
                  pl.BlockSpec((1, 8, width), lambda g, k: (g, jnp.maximum((last - k) * (step // 8) - 1, 0), 0)), few,
                  whole(taps.shape), whole((1, width)), few] + free,
        out_specs=[rows, few, few, pl.BlockSpec((1, sums, width), lambda g, k: (g, 0, 0))],
        scratch_shapes=[pltpu.VMEM((step, width), F32), pltpu.VMEM((step + 8, width), F32), pltpu.VMEM((step + 8, width), F32)],
        input_output_aliases=alias, compiler_params=params(), cost_estimate=cost(0.2), name="conv_back",
    )(d_proj, xproj_t, d_mix, inner_x, inner_x, rim, taps, shift, carry, *kept)


def place_kernel(doc_ref, *refs, pieces):
    parts, (weight_ref, gain_ref, sum_ref) = refs[:pieces], refs[pieces:pieces + 3]
    out_ref, total_ref = refs[-2:]
    j = pl.program_id(0)

    def put(x):
        x = x.astype(F32)
        out_ref[...] = x * gain_ref[...]
        x = x * weight_ref[...].astype(F32)
        x = sum(x[:, c:c + 128] for c in range(0, x.shape[1], 128))
        total_ref[...] = jnp.where(j == 0, sum_ref[...], total_ref[...]) + x

    if pieces == 1:
        put(parts[0][...])
    else:
        for p in range(pieces):
            @pl.when(j == p)
            def _():
                put(parts[p][...])


def place(doc, kept, parts, weight, gain, sums, block, offset):
    rows, width = weight.shape
    docs = width // 2 // block
    at = (lambda j, doc_ref: (0, offset + j)) if len(parts) == 1 else (lambda j, doc_ref: (0, offset + (doc_ref[0] ^ j)))
    one = lambda j, doc_ref: (0, 0)
    piece_at = (lambda j, doc_ref: (0, j)) if len(parts) == 1 else one
    free = [pl.BlockSpec(memory_space=pl.ANY)] * len(kept)
    return pl.pallas_call(
        functools.partial(place_kernel, pieces=len(parts)),
        out_shape=[shape((rows, width)), shape((rows, 128))],
        grid_spec=pltpu.PrefetchScalarGridSpec(
            num_scalar_prefetch=1, grid=(docs,),
            in_specs=[pl.BlockSpec((rows, block), piece_at)] * len(parts)
            + [pl.BlockSpec((rows, block), at), pl.BlockSpec((rows, 1), one), pl.BlockSpec((rows, 128), one)] + free,
            out_specs=[pl.BlockSpec((rows, block), at), pl.BlockSpec((rows, 128), one)]),
        input_output_aliases={4 + len(parts): 0} if kept else {},
        compiler_params=params(), cost_estimate=cost(0.1), name="place",
    )(doc, *parts, weight, gain, sums, *kept)


def input_kernel(part_ref, one_ref, two_ref, hidden_ref, cot_ref, out_ref):
    d_normed = part_ref[...] + one_ref[...].astype(F32) + two_ref[...].astype(F32)
    r = hidden_ref[...].astype(F32)
    scale = lax.rsqrt(jnp.mean(r * r, axis=1, keepdims=True) + NORM_EPS)
    scaled = r * scale
    out_ref[...] = cot_ref[...].astype(F32) + scale * (d_normed - scaled * jnp.mean(d_normed * scaled, axis=1, keepdims=True))


def input_gradient(part, one, two, hidden, cot, step=128):
    rows = pl.BlockSpec((step, hidden.shape[1]), lambda k: (k, 0))
    return pl.pallas_call(
        input_kernel, out_shape=shape(hidden.shape), grid=(hidden.shape[0] // step,),
        in_specs=[rows] * 5, out_specs=rows, compiler_params=params(), cost_estimate=cost(0.1), name="input_gradient",
    )(part, one, two, hidden, cot)


def shifted(block, axis, distance):
    devices = range(lax.axis_size(axis))
    route = [(i - distance, i) for i in devices if i - distance in devices]
    return lax.ppermute(block, axis, route)


def swap(x, axis, flip):
    return lax.ppermute(x, axis, [(i, i ^ flip) for i in range(lax.axis_size(axis))])


def piece(x, index, size, axis):
    return lax.dynamic_slice_in_dim(x, index * size, size, axis)


def chain(decays, states, order, keep, start):
    state = start
    for k in order:
        decay = decays[k].astype(F32)
        state = jnp.where(keep(k), decay * state + states[k].astype(F32), state)
    return state


def doc_gather(x):
    return [x] + [swap(x, "doc", j) for j in (1, 2, 3)]


def doc_sum(parts):
    total = parts[0].astype(F32)
    for j in (1, 2, 3):
        total = total + swap(parts[j].astype(BF), "doc", j).astype(F32)
    return total


def doc_place(parts, doc, axis):
    stack = jnp.stack(parts)
    return jnp.concatenate([lax.dynamic_index_in_dim(stack, doc ^ k, 0, False) for k in range(len(parts))], axis=axis)


def shards(hidden_in, cotangent, scan_init, conv_init, norm_gain, in_weight, conv_weight, conv_bias,
           xproj_weight, dt_weight, dt_bias, a_log, skip_d, out_weight):
    docs, seqs = lax.axis_size("doc"), lax.axis_size("seq")
    doc, seq = lax.axis_index("doc"), lax.axis_index("seq")
    near = seqs == 2 * docs == 8
    hidden, cot = hidden_in[0], cotangent[0]
    tokens, width = hidden.shape
    inner = in_weight.shape[1] // 2
    rank = dt_weight.shape[0]
    states = a_log.shape[0]
    lead = conv_init.shape[1]
    taps = conv_weight.shape[0]
    block = inner // docs
    rows_all = docs * tokens
    blocks = tokens // TB
    middle = tokens // 2
    slots = range(docs)

    def mine(x, offset=0):
        return lax.dynamic_slice_in_dim(x, offset + doc * block, block, x.ndim - 1)

    def mine_of(x, owner):
        return piece(x, owner, block, 1)

    def seq_gather(x):
        return lax.all_gather(x, "seq", axis=0, tiled=True)

    state_rows, lead_rows = states * block // width, 2 * (-(-lead * block // (2 * width)))

    def first_of(j):
        rows = mine_of(conv_init[0], doc ^ j)
        rows = jnp.pad(rows, ((0, lead_rows * width // block - lead), (0, 0))).reshape(lead_rows, width)
        start = mine_of(scan_init[0], doc ^ j).astype(BF).reshape(state_rows, width)
        packed = jnp.concatenate([hidden[tokens - 16:], start, rows], axis=0)
        return jnp.pad(packed, ((0, 32 - packed.shape[0]), (0, 0)))

    halo = [lax.ppermute(first_of(j), ("doc", "seq"),
                         [(d * seqs + s, (d ^ j) * seqs + (s + 1) % seqs) for d in slots for s in range(seqs)])
            for j in slots]
    top, low = hidden[:middle], tie(hidden[middle:], *halo)
    one, two = ([swap(x, "doc", j) for x in (top, low)] for j in (1, 2))
    scaled_weight = (in_weight.astype(F32) * norm_gain.astype(F32)[:, None]).astype(BF)
    w_inner = seq_gather(mine(scaled_weight))
    few = jnp.concatenate([conv_weight, conv_bias[None], dt_bias[None], skip_d[None]], axis=0)
    few = jnp.pad(few, ((0, 16 - few.shape[0]), (0, 0)))
    small = jnp.concatenate([few, a_log, dt_weight, xproj_weight.T], axis=0)
    if near:
        route = [((d, 2 * z + c), (z, 2 * d + c)) for d in slots for z in slots for c in range(2)]
        turn = [(a * seqs + b, e * seqs + f) for (a, b), (e, f) in route]
        half = lax.ppermute(small, ("doc", "seq"), turn)
        half = tie(half, *one, *two)
        other = swap(half, "seq", 1)
        core = seq % 2 == 0
        small = jnp.concatenate([jnp.where(core, half, other), jnp.where(core, other, half)], axis=1)
    else:
        small = mine(lax.all_gather(small, "seq", axis=1, tiled=True))
    three = [swap(two[0], "doc", 1), swap(one[1], "doc", 2)]
    w_gate = seq_gather(tie(mine(scaled_weight, inner), small))
    w_out = seq_gather(mine(out_weight))

    wide = small.astype(F32)
    conv_taps, conv_shift, dt_shift, skip = wide[:taps], wide[taps][None], wide[taps + 1][None], wide[taps + 2][None]
    at = 16
    rate = -jnp.exp(wide[at:at + states])
    dt_full = small[at + states:at + states + rank]
    xproj_t = small[at + states + rank:]
    rate2 = rate * (1.0 / LN2)

    is_first = (seq == 0).astype(jnp.int32)[None]

    def first_rows(x):
        rows = x[16 + state_rows:16 + state_rows + lead_rows].reshape(-1, block)[:lead].astype(F32)
        return jnp.pad(rows, ((8 - lead, 0), (0, 0)))

    kept, proj_part = (), []
    for j, x in enumerate(((top, low), one, two, three)):
        if j == 3:
            x = [tie(half, kept[0]) for half in three]
            cot_top = tie(cot[:middle], *x)
            cot_near = [swap(cot_top, "doc", 1), swap(cot_top, "doc", 2)]
        *kept, part = front(j, docs, kept, is_first, *x, halo[j], w_inner, small, lead,
                            rank + 2 * states, first_rows(halo[j]))
        proj_part.append(part)
    normed, inner_x, mixed, rim = kept
    mixed_flat = mixed.reshape(rows_all, block)

    w_gate = tie(w_gate, *proj_part)
    gate_in = mm(normed, w_gate)
    got = [tie(swap(proj_part[j].astype(BF), "doc", j), gate_in) for j in slots[1:]]
    proj_own = (proj_part[0] + sum(x.astype(F32) for x in got)).astype(BF)
    proj = jnp.concatenate(doc_gather(proj_own), axis=0)
    proj = tie(proj, *cot_near)
    cot_low = tie(cot[middle:], proj)
    cot_rest = [swap(cot_low, "doc", 1), swap(cot_low, "doc", 2)]
    cot_far = [swap(tie(cot_near[1], proj), "doc", 1)]
    init = jnp.stack([x[16:16 + state_rows].reshape(states, block) for x in halo]).astype(F32)
    rank_in = proj[:, :rank]
    gate_in = gate_in.reshape(docs, tokens, block)

    mask = jnp.repeat(jnp.eye(TB, dtype=F32), states, axis=1)
    spread = jnp.tile(jnp.eye(states, dtype=BF), (1, TB))

    def columns(x):
        return jnp.swapaxes(x.reshape(docs, blocks, TB, states), 2, 3).astype(F32)

    def diagonal(x):
        return (mm(x, spread).reshape(docs, blocks, TB, TB * states) * mask).astype(BF)

    b_rows, c_rows = proj[:, rank:rank + states], proj[:, rank + states:]
    b_cols, c_cols = columns(b_rows), columns(c_rows)
    b_diag, c_diag = diagonal(b_rows), diagonal(c_rows)

    rank_in = rank_in.reshape(docs, tokens, rank)
    part = docs // 2
    starts, decays = {}, {}
    kept = ()
    for base in (part, 0):
        *kept, end_state, decay = summary(base, part, kept, rank_in, dt_full, dt_shift, mixed, b_cols, rate2)
        if base == 0:
            end_state = tie(end_state, *cot_far)
        ends = lax.all_gather(jnp.stack([end_state, decay]).astype(BF), "seq")
        decays[base] = ends[:, 1]
        starts[base] = chain(ends[:, 1], ends[:, 0], range(seqs), lambda k: k < seq, init[base:base + part])
        if base:
            cot_far.append(swap(tie(cot_rest[0], end_state), "doc", 2))
            kept[0] = tie(kept[0], cot_rest[0], w_out)
    dt_pre, delta = kept
    rank_in = rank_in.reshape(rows_all, rank)

    cot_all = jnp.concatenate([cot_top, cot_low, cot_near[0], cot_rest[0], cot_near[1], cot_rest[1], *cot_far], axis=0)
    cot_all = tie(cot_all, end_state)
    def relay_far(x):
        x, half = x.astype(BF), x.shape[0] // 32 * 16
        return swap(x[:half], "doc", 1), swap(x[half:], "doc", 2)

    def relay_near(parts, one, two):
        half = one.shape[0]
        first = jnp.concatenate([parts[1][:half], parts[1][half:] + two.astype(F32)], axis=0).astype(BF)
        second = jnp.concatenate([parts[2][:half] + one.astype(F32), parts[2][half:]], axis=0).astype(BF)
        return first, second

    d_start, skip_grad, out_rows = {}, [], {}
    kept = ()
    for base in (part, 0):
        rows = slice(base * tokens, (base + part) * tokens)
        d_gated = mm(cot_all[rows], w_out).reshape(part, tokens, block)
        if base == 0:
            d_gated = tie(d_gated, *out_rows.values())
        *kept, d_start[base], skip_part = forward(base, part, kept, delta, mixed, gate_in, d_gated, b_cols, c_diag, rate2,
                                                  starts[base], mask, skip)
        skip_grad.append(skip_part)
        for j in range(base + part - 1, base - 1, -1):
            out_rows[j] = mm_last(kept[2][j], w_out)
        if base:
            out_far = relay_far(out_rows[3])
    out_far = [tie(x, d_start[0]) for x in out_far]
    d_y, before, gated, d_gate, d_out = kept
    gated, d_gate = gated.reshape(rows_all, block), d_gate.reshape(rows_all, block)
    skip_grad = sum(jnp.sum(x, axis=(0, 1)) for x in skip_grad)
    later = lax.all_gather(jnp.concatenate([d_start[0], d_start[part]], axis=0).astype(BF), "seq")
    decays = jnp.concatenate([decays[0], decays[part]], axis=1)
    zero = jnp.zeros((docs, states, block), F32)
    back = range(seqs - 1, -1, -1)
    later_sum = chain(decays, later, back, lambda k: k > seq, zero)
    first_sum = chain(decays, later, back, lambda k: True, zero)

    def seq_sum(x):
        return lax.psum_scatter(x, "seq", scatter_dimension=0, tiled=True)

    def all_blocks(total):
        return lax.all_gather(total, "doc", axis=1, tiled=True)

    out_first, out_second = relay_near(out_rows, *out_far)
    out_got = swap(out_first, "doc", 1), swap(out_second, "doc", 2)
    gated = tie(gated, out_first, out_second)
    out_part = mm_first(cot_all, gated).astype(BF)
    gate_part = mm_first(normed, d_gate).astype(BF)
    later_sum = tie(later_sum, out_part, gate_part)
    out_part, gate_part = seq_sum(out_part), seq_sum(gate_part)

    d_out = d_out.reshape(docs, tokens, states)

    def proj_parts(kept, begin):
        rows = slice(begin, begin + middle)
        d_rank = mm_last(kept[0][:, rows].reshape(docs * middle, block), dt_full).reshape(docs, middle, rank)
        d_in = kept[2].reshape(docs, tokens, states)[:, rows]
        full = jnp.concatenate([d_rank, d_in, d_out[:, rows]], axis=2)
        return full[0], [full[j].astype(BF) for j in slots[1:]]

    def run_back(begin, kept, state):
        return backward(0, docs, begin, kept, dt_pre, delta, mixed, d_y, before, c_cols, b_diag, rate2, state, mask, skip)

    *kept, rate_grad, dt_bias_grad, passed_on = run_back(middle, (), later_sum)
    kept[0] = tie(kept[0], *out_got)
    out_got = [tie(x, kept[2]) for x in out_got]
    out_total = all_blocks(tie(out_part, kept[2]))
    own_late, sent = proj_parts(kept, middle)
    got = [swap(x, "doc", j) for j, x in zip(slots[1:], sent)]
    kept[0] = tie(kept[0], *sent)
    *kept, rate_part, bias_part, _ = run_back(0, kept, passed_on)
    got = [tie(x, kept[2]) for x in got]
    own_late = (own_late + sum(x.astype(F32) for x in got)).astype(BF)
    kept[0] = tie(kept[0], own_late, out_total)
    gate_total = all_blocks(tie(gate_part, kept[2]))
    late = [own_late] + [swap(own_late, "doc", j) for j in slots[1:]]
    d_pre, d_mix, _ = kept
    rate_grad = jnp.sum(rate_grad + rate_part, axis=0)
    dt_bias_grad = jnp.sum(dt_bias_grad + bias_part, axis=(0, 1))
    own_early, sent = proj_parts(kept, 0)
    got = [swap(x, "doc", j) for j, x in zip(slots[1:], sent)]

    nothing = jnp.zeros((docs, 8, block), F32)
    d_proj_late = tie(jnp.stack(late), *sent)
    d_inner, tail, carry, sums_late = conv_back(middle, (), nothing, d_proj_late, xproj_t, d_mix, inner_x, rim, conv_taps,
                                                conv_shift)
    d_gate = tie(d_gate, *sent).reshape(docs, tokens, block)
    gate_far = mm_last(d_gate[3], w_gate)
    own_early = (own_early + sum(x.astype(F32) for x in got)).astype(BF)
    d_inner = tie(d_inner, own_early)
    early = [own_early] + [swap(own_early, "doc", j) for j in slots[1:]]

    d_inner = tie(d_inner, gate_far, *early[1:])
    d_proj_early = jnp.stack(early)
    d_proj = jnp.concatenate([d_proj_early, d_proj_late], axis=1).reshape(rows_all, -1)
    few = jnp.concatenate([rate_grad, dt_bias_grad[None], skip_grad[None], jnp.zeros((14, block), F32)], axis=0)
    small_grad = [few, mm_first(rank_in, d_pre.reshape(rows_all, block)),
                  mm_first(d_proj, mixed_flat)]
    if near:
        side = seq % 2
        small_sum, sent = (jnp.concatenate([piece(x, at_side, block // 2, 1) for x in small_grad], axis=0)
                           for at_side in (side, 1 - side))
        small_sum = (small_sum + swap(sent.astype(BF), "seq", 1).astype(F32)).astype(BF)
        turned = lax.ppermute(small_sum, ("doc", "seq"), turn)
        d_proj_early = tie(d_proj_early, small_sum, gate_total)
    else:
        small_grad = jnp.concatenate(small_grad, axis=0)
        small_sum = lax.psum_scatter(small_grad, "seq", scatter_dimension=1, tiled=True)
        small_sum = lax.all_gather(small_sum.astype(BF), ("doc", "seq"), axis=1, tiled=True)
        turned = piece(small_sum, seq, inner // seqs, 1).astype(F32)

    d_inner, _, head, sums = conv_back(0, [d_inner], carry, d_proj_early, xproj_t, d_mix, inner_x, rim, conv_taps, conv_shift)
    d_ext = jnp.stack([sum(conv_taps[k] * head[:, j - k] for k in range(j + 1)) for j in range(lead)], axis=1)
    passed = shifted(d_ext.astype(BF), "seq", -1).astype(F32)
    d_inner = lax.dynamic_update_slice(d_inner, (tail[:, 8 - lead:] + passed).astype(BF), (0, tokens - lead, 0))
    d_inner = tie(d_inner, turned)
    inner_part = mm_first(normed, d_inner.reshape(rows_all, block)).astype(BF)
    d_inner = tie(d_inner, inner_part)
    inner_part = seq_sum(inner_part)
    small_sum = sum(x.astype(F32) for x in doc_gather(turned)) if near else turned
    d_inner = tie(d_inner, small_sum)

    d_gate = tie(d_gate, d_inner)

    def normed_part(j):
        return mm_last(d_inner[j], w_inner) + mm_last(d_gate[j], w_gate)

    far = mm_last(d_inner[3], w_inner) + gate_far
    far_got = relay_far(far)
    d_inner = tie(d_inner, far)
    parts = [normed_part(j) for j in range(3)]
    first, second = relay_near(parts, *(tie(x, parts[0]) for x in far_got))
    early_got = swap(first, "doc", 1), swap(second, "doc", 2)
    inner_total = all_blocks(tie(inner_part, first, second))
    gain = norm_gain.astype(F32)[:, None]
    in_total, gain_sum = place(doc[None], [], [gate_total], in_weight, gain, jnp.zeros((width // seqs, 128), F32), block, docs)

    output = (hidden.astype(F32) + out_rows[0] + sum(x.astype(F32) for x in out_got)).astype(BF)
    sums = jnp.sum((sums + sums_late).reshape(docs, taps + 1, 8, block), axis=(0, 2))
    ends = jnp.concatenate([jnp.where(seq == 0, tie(d_ext, *early_got, inner_part), 0.0).reshape(docs * lead, block), sums], axis=0)
    if near:
        for flip in (1, 2, 4):
            ends = ends + swap(ends, "seq", flip)
    else:
        ends = lax.psum(ends, "seq")
    sends = [jnp.concatenate([first_sum[j], ends[j * lead:(j + 1) * lead], ends[docs * lead:]], axis=0) for j in slots]
    ends = doc_place([sends[0]] + [swap(sends[j], "doc", j) for j in slots[1:]], doc, 1)
    init_grad, conv_sum = ends[:states + lead], piece(ends[states + lead:], seq, inner // seqs, 1)
    input_grad = input_gradient(parts[0], *early_got, hidden, cot)
    in_total, gain_sum = place(doc[None], [in_total], [inner_total], in_weight, gain, gain_sum, block, 0)
    gain_sum = jnp.sum(gain_sum, axis=1)

    return (
        output[None],
        input_grad[None],
        init_grad[None, :states],
        init_grad[None, states:],
        gain_sum,
        in_total,
        conv_sum[1:],
        conv_sum[0],
        small_sum[states + 16 + rank:].T,
        small_sum[states + 16:states + 16 + rank],
        small_sum[states],
        small_sum[:states],
        small_sum[states + 1],
        out_total.astype(F32),
    )


def solution(mesh):
    placed = (
        P("doc", "seq", None), P("doc", "seq", None), P("doc", None, None), P("doc", None, None),
        P("seq"), P("seq", None), P(None, "seq"), P("seq"), P("seq", None), P(None, "seq"),
        P("seq"), P(None, "seq"), P("seq"), P("seq", None),
    )
    return jax.shard_map(shards, mesh=mesh, in_specs=placed, out_specs=placed, check_vma=False)
```

```python
import functools
import jax
import jax.numpy as jnp
from jax import lax
from jax.experimental import pallas as pl
from jax.experimental.pallas import tpu as pltpu
from jax.sharding import PartitionSpec as P

TB = 16
F32 = jnp.float32
BF = jnp.bfloat16
LN2 = 0.6931471805599453
NORM_EPS = 1e-05
LAST = (((1,), (1,)), ((), ()))
FIRST = (((0,), (0,)), ((), ()))


def mm(a, b):
    return jnp.dot(a, b, preferred_element_type=F32)


def mm_last(a, b):
    return lax.dot_general(a, b, LAST, preferred_element_type=F32)


def mm_first(a, b):
    return lax.dot_general(a, b, FIRST, preferred_element_type=F32)


def cost(us):
    return pl.CostEstimate(flops=int(us * 1.0e9), bytes_accessed=0, transcendentals=0)


def params():
    return pltpu.CompilerParams(vmem_limit_bytes=56 * 2**20)


def shape(dims, kind=F32):
    return jax.ShapeDtypeStruct(dims, kind)


def whole(dims):
    return pl.BlockSpec(dims, lambda *_: (0,) * len(dims))


def tie(x, *tokens):
    free = pl.BlockSpec(memory_space=pl.ANY)
    return pl.pallas_call(lambda *refs: None, out_shape=shape(x.shape, x.dtype),
                          in_specs=[free] * (1 + len(tokens)), out_specs=free, input_output_aliases={0: 0},
                          name="tie")(x, *tokens)


def sigmoid(x):
    return 0.5 + 0.5 * jnp.tanh(0.5 * x)


def tiles(x):
    return sum(x[:, c:c + 128] for c in range(0, x.shape[1], 128))


def softplus(x):
    return jnp.maximum(x, 0.0) + jnp.log1p(jnp.exp(-jnp.abs(x)))


def front_kernel(first_ref, top_ref, low_ref, halo_ref, w_ref, few_ref, xproj_ref, init_ref, *refs, lead):
    taps, shift = few_ref[:lead + 1].astype(F32), few_ref[lead + 1:lead + 2].astype(F32)
    normed_ref, inner_ref, mixed_ref, rim_ref, proj_ref, xs_ref = refs[-6:]
    step, width = top_ref.shape[0], xs_ref.shape[1]

    def normalise(x):
        r = x.astype(F32)
        scale = lax.rsqrt(jnp.mean(r * r, axis=1, keepdims=True) + NORM_EPS)
        return (r * scale).astype(BF)

    @pl.when(pl.program_id(0) == 0)
    def _():
        before = mm(normalise(halo_ref[...]), w_ref[...])[halo_ref.shape[0] - 8:]
        rim = jnp.where(first_ref[0] == 1, init_ref[...], before)
        rim_ref[0] = rim
        xs_ref[:8] = rim

    in_top = 2 * pl.program_id(0) < pl.num_programs(0)
    normed_ref[...] = normalise(jnp.where(in_top, top_ref[...], low_ref[...]))
    x = mm(normed_ref[...], w_ref[...])
    inner_ref[0] = x
    xs_ref[8:] = x
    for c in range(0, width, 256):
        cs = pl.ds(c, 256)
        pre = shift[:, c:c + 256]
        for tap in range(lead + 1):
            pre = pre + taps[tap:tap + 1, c:c + 256] * xs_ref[pl.ds(8 - lead + tap, step), cs]
        mixed_ref[0, :, cs] = (pre * sigmoid(pre)).astype(BF)
    proj_ref[...] = mm_last(mixed_ref[0], xproj_ref[...])
    xs_ref[:8] = xs_ref[step:step + 8]


def front(slot, docs, kept, first, top, low, halo, w, small, lead, cols, init, step=128):
    width, block = w.shape
    extra = 16
    tokens = 2 * top.shape[0]
    count = tokens // step
    rows = pl.BlockSpec((1, step, block), lambda k: (slot, k, 0))
    few = pl.BlockSpec((1, 8, block), lambda k: (slot, 0, 0))
    return pl.pallas_call(
        functools.partial(front_kernel, lead=lead),
        out_shape=[shape((docs * tokens, width), BF), shape((docs, tokens, block)), shape((docs, tokens, block), BF),
                   shape((docs, 8, block)), shape((tokens, cols))],
        grid=(count,),
        in_specs=[pl.BlockSpec(memory_space=pltpu.SMEM), pl.BlockSpec((step, width), lambda k: (jnp.minimum(k, count // 2 - 1), 0)),
                  pl.BlockSpec((step, width), lambda k: (jnp.maximum(k - count // 2, 0), 0)),
                  pl.BlockSpec((extra, width), lambda k: (0, 0)), whole(w.shape),
                  whole((16, block)), pl.BlockSpec((cols, block), lambda k: (1, 0)), whole((8, block))]
        + [pl.BlockSpec(memory_space=pl.ANY)] * len(kept),
        out_specs=[pl.BlockSpec((step, width), lambda k: (slot * count + k, 0)), rows, rows, few,
                   pl.BlockSpec((step, cols), lambda k: (k, 0))],
        scratch_shapes=[pltpu.VMEM((step + 8, block), F32)],
        input_output_aliases={8 + i: i for i in range(len(kept))},
        compiler_params=params(), cost_estimate=cost(0.1), name="front",
    )(first, top, low, halo, w, small, small, init, *kept)


def summary_kernel(rank_ref, dtw_ref, shift_ref, mixed_ref, bt_ref, rate_ref, *refs):
    pre_ref, delta_ref, end_ref, decay_ref = refs[-4:]
    tokens, width = mixed_ref.shape[1:]
    rate = rate_ref[...]
    group = 4
    count = tokens // (TB * group)

    def steps(i):
        rows = pl.ds(pl.multiple_of(i * TB * group, TB * group), TB * group)
        pre = mm(rank_ref[0, rows], dtw_ref[...]) + shift_ref[...]
        pre_ref[0, rows] = pre
        delta_ref[0, rows] = softplus(pre)

    steps(0)

    def body(i, carry):
        h, total = carry
        for b in range(group):
            rows = pl.ds(pl.multiple_of((i * group + b) * TB, TB), TB)
            dl = delta_ref[0, rows]
            dr = dl * mixed_ref[0, rows].astype(F32)
            bt = bt_ref[0, i * group + b]
            for t in range(TB):
                h = jnp.exp2(dl[t:t + 1] * rate) * h + bt[:, t:t + 1] * dr[t:t + 1]
            total = total + dl
        steps(jnp.minimum(i + 1, count - 1))
        return h, total

    h, total = lax.fori_loop(0, count, body, (jnp.zeros(rate.shape, F32), jnp.zeros((TB, width), F32)))
    end_ref[0] = h
    decay_ref[0] = jnp.exp2(jnp.sum(total, axis=0, keepdims=True) * rate)


def chained(kept, before):
    return [pl.BlockSpec(memory_space=pl.ANY)] * len(kept), {before + i: i for i in range(len(kept))}


def summary(base, count, kept, rank_in, dtw, shift, mixed, bt, rate):
    docs, tokens, width = mixed.shape
    n, rank = rate.shape[0], rank_in.shape[2]
    rows = pl.BlockSpec((1, tokens, width), lambda g: (g + base, 0, 0))
    state = pl.BlockSpec((1, n, width), lambda g: (g, 0, 0))
    free, alias = chained(kept, 6)
    return pl.pallas_call(
        summary_kernel,
        out_shape=[shape((docs, tokens, width))] * 2 + [shape((count, n, width))] * 2,
        grid=(count,),
        in_specs=[pl.BlockSpec((1, tokens, rank), lambda g: (g + base, 0, 0)), whole(dtw.shape), whole((1, width)), rows,
                  pl.BlockSpec((1, tokens // TB, n, TB), lambda g: (g + base, 0, 0, 0)), whole(rate.shape)] + free,
        out_specs=[rows, rows, state, state], input_output_aliases=alias,
        compiler_params=params(), cost_estimate=cost(22), name="summary",
    )(rank_in, dtw, shift, mixed, bt, rate, *kept)


def forward_kernel(delta_ref, mixed_ref, gate_ref, dg_ref, bt_ref, cdiag_ref, rate_ref, start_ref, mask_ref, skip_ref,
                   *refs):
    dy_ref, before_ref, gated_ref, dgate_ref, dout_ref, dstart_ref, sgrad_ref, hs_ref, ps_ref, hb_ref, zb_ref, sb_ref, sig_ref = refs[-13:]
    tokens = delta_ref.shape[1]
    n = rate_ref.shape[0]
    count = tokens // TB
    rate = rate_ref[...]

    @pl.when(pl.program_id(1) == 0)
    def _():
        hs_ref[...] = start_ref[0]
        ps_ref[...] = jnp.ones_like(ps_ref)
        dstart_ref[0] = jnp.zeros(dstart_ref.shape[1:], F32)
        sgrad_ref[0] = jnp.zeros(sgrad_ref.shape[1:], F32)

    mask = mask_ref[...]
    spread = lax.rem(lax.broadcasted_iota(jnp.int32, mask.shape, 1), n) == lax.broadcasted_iota(jnp.int32, mask.shape, 0)

    def finish(i, hm, good):
        rows = pl.ds(pl.multiple_of(i * TB, TB), TB)
        gate, dg, sig = gate_ref[0, rows], dg_ref[0, rows], sig_ref[...]
        act = gate * sig
        mx = mixed_ref[0, rows].astype(F32)
        y = mm(cdiag_ref[0, i], hm) + skip_ref[...] * mx
        gated_ref[0, rows] = (y * act).astype(BF)
        dgate_ref[0, rows] = (dg * y * (sig * (1.0 + gate * (1.0 - sig)))).astype(BF)
        dout_ref[0, i] = mm_last(jnp.ones((8, 128), BF), sb_ref[...])[:1]
        weight = jnp.where(spread, jnp.sum(cdiag_ref[0, i].astype(F32), axis=0, keepdims=True), 0.0).astype(BF)
        dstart_ref[0] += jnp.where(good, mm(weight, zb_ref[...]), 0.0)

    def body(i, carry):
        h, p = carry
        rows = pl.ds(pl.multiple_of(i * TB, TB), TB)
        dl = delta_ref[0, rows]
        mx = mixed_ref[0, rows].astype(F32)
        dr = dl * mx
        gate = gate_ref[0, rows]
        sig = sigmoid(gate)
        dy = dg_ref[0, rows] * (gate * sig)
        dy_ref[0, rows] = dy
        sgrad_ref[0] += dy * mx
        bt = bt_ref[0, i]
        hb = h.astype(BF)
        before_ref[0, pl.ds(pl.multiple_of(i * TB * n, TB * n), n)] = hb
        last = jnp.maximum(i - 1, 0)
        finish(last, before_ref[0, pl.ds(pl.multiple_of((last * TB + 1) * n, n), TB * n)], i > 0)
        sig_ref[...] = sig
        for t in range(TB):
            if t:
                before_ref[0, pl.ds(pl.multiple_of((i * TB + t) * n, n), n)] = hb
            a = jnp.exp2(dl[t:t + 1] * rate)
            h = a * h + bt[:, t:t + 1] * dr[t:t + 1]
            hb = h.astype(BF)
            sb_ref[t * n:(t + 1) * n] = tiles(h * dy[t:t + 1]).astype(BF)
            p = p * a
            zb_ref[t * n:(t + 1) * n] = (p * dy[t:t + 1]).astype(BF)
        return h, p

    h, p = lax.fori_loop(0, count, body, (hs_ref[...], ps_ref[...]))
    hs_ref[...] = h
    ps_ref[...] = p
    hb_ref[:(TB - 1) * n] = before_ref[0, ((count - 1) * TB + 1) * n:count * TB * n]
    hb_ref[(TB - 1) * n:] = h.astype(BF)
    finish(count - 1, hb_ref[...], True)


def forward(base, part, kept, delta, mixed, gate, d_gated, bt, cdiag, rate, start, mask, skip, step=128):
    docs, tokens, width = delta.shape
    n, nb = rate.shape[0], step // TB
    rows = pl.BlockSpec((1, step, width), lambda g, k: (g + base, k, 0))
    own = pl.BlockSpec((1, step, width), lambda g, k: (g, k, 0))
    state = pl.BlockSpec((1, n, width), lambda g, k: (g, 0, 0))
    cols = pl.BlockSpec((1, nb, n, TB), lambda g, k: (g + base, k, 0, 0))
    free, alias = chained(kept, 10)
    return pl.pallas_call(
        forward_kernel,
        out_shape=[shape(delta.shape), shape((docs, tokens * n, width), BF), shape(delta.shape, BF), shape(delta.shape, BF),
                   shape((docs, tokens // TB, 1, TB * n)), shape((part, n, width)), shape((part, TB, width))],
        grid=(part, tokens // step),
        in_specs=[rows, rows, rows, own, cols, pl.BlockSpec((1, nb, TB, TB * n), lambda g, k: (g + base, k, 0, 0)),
                  whole(rate.shape), state, whole(mask.shape), whole((1, width))] + free,
        out_specs=[rows, pl.BlockSpec((1, step * n, width), lambda g, k: (g + base, k, 0)), rows, rows,
                   pl.BlockSpec((1, nb, 1, TB * n), lambda g, k: (g + base, k, 0, 0)), state,
                   pl.BlockSpec((1, TB, width), lambda g, k: (g, 0, 0))],
        scratch_shapes=[pltpu.VMEM((n, width), F32), pltpu.VMEM((n, width), F32), pltpu.VMEM((TB * n, width), BF),
                        pltpu.VMEM((TB * n, width), BF), pltpu.VMEM((TB * n, 128), BF), pltpu.VMEM((TB, width), F32)],
        input_output_aliases=alias, compiler_params=params(), cost_estimate=cost(45), name="forward",
    )(delta, mixed, gate, d_gated, bt, cdiag, rate, start, mask, skip, *kept)


def backward_kernel(pre_ref, delta_ref, mixed_ref, dy_ref, before_ref, ct_ref, bdiag_ref, rate_ref, qin_ref, mask_ref, skip_ref,
                    *refs):
    dpre_ref, dmix_ref, din_ref, drate_ref, bgrad_ref, qout_ref, ps_ref, qb_ref, wb_ref, sb_ref = refs[-10:]
    tokens = delta_ref.shape[1]
    n = rate_ref.shape[0]
    count = tokens // TB
    rate = rate_ref[...]

    @pl.when(pl.program_id(1) == 0)
    def _():
        ps_ref[...] = qin_ref[0]
        drate_ref[0] = jnp.zeros(drate_ref.shape[1:], F32)
        bgrad_ref[0] = jnp.zeros(bgrad_ref.shape[1:], F32)

    mask = mask_ref[...]
    spread = lax.rem(lax.broadcasted_iota(jnp.int32, mask.shape, 1), n) == lax.broadcasted_iota(jnp.int32, mask.shape, 0)
    sums = jnp.concatenate([mask, spread.astype(F32)], axis=0).astype(BF)

    fold = jnp.ones((8, 128), BF)

    def finish(i, good, side):
        rows = pl.ds(pl.multiple_of(i * TB, TB), TB)
        dl = delta_ref[0, rows]
        mx = mixed_ref[0, rows].astype(F32)
        d_drive = mm(bdiag_ref[0, i], qb_ref[side])
        both = LN2 * mm(sums, wb_ref[side])
        din_ref[0, i] = mm_last(fold, sb_ref[side])[:1]
        drate_ref[0] += jnp.where(good, both[TB:], 0.0)
        sig = sigmoid(pre_ref[0, rows])
        d_pre = both[:TB] * jnp.where(dl > 1e-30, sig / dl, 1.0) + mx * d_drive * sig
        dpre_ref[0, rows] = d_pre.astype(BF)
        bgrad_ref[0] += jnp.where(good, d_pre, 0.0)
        dmix_ref[0, rows] = dl * d_drive + dy_ref[0, rows] * skip_ref[...]

    def scan(i, p, side):
        rows = pl.ds(pl.multiple_of(i * TB, TB), TB)
        dl = delta_ref[0, rows]
        dr = dl * mixed_ref[0, rows].astype(F32)
        dy = dy_ref[0, rows]
        ct = ct_ref[0, i]
        for t in reversed(range(TB)):
            q = ct[:, t:t + 1] * dy[t:t + 1] + p
            qb_ref[side, t * n:(t + 1) * n] = q.astype(BF)
            sb_ref[side, t * n:(t + 1) * n] = tiles(q * dr[t:t + 1]).astype(BF)
            x = dl[t:t + 1] * rate
            p = jnp.exp2(x) * q
            e = p * before_ref[0, pl.ds(pl.multiple_of((i * TB + t) * n, n), n)].astype(F32)
            wb_ref[side, t * n:(t + 1) * n] = (x * e).astype(BF)
        return p

    def body(j, p):
        i = count - 1 - 2 * j
        finish(jnp.minimum(i + 1, count - 1), j > 0, 1)
        p = scan(i, p, 0)
        finish(i, True, 0)
        return scan(i - 1, p, 1)

    ps_ref[...] = lax.fori_loop(0, count // 2, body, ps_ref[...])
    finish(0, True, 1)
    qout_ref[0] = ps_ref[...]


def backward(base, part, begin, kept, pre, delta, mixed, dy, before, ct, bdiag, rate, qin, mask, skip, step=128):
    docs, tokens, width = delta.shape
    n, nb, last = rate.shape[0], step // TB, (begin + tokens // 2) // step - 1
    rows = pl.BlockSpec((1, step, width), lambda g, k: (g + base, last - k, 0))
    state = pl.BlockSpec((1, n, width), lambda g, k: (g, 0, 0))
    line = pl.BlockSpec((1, nb, 1, TB * n), lambda g, k: (g + base, last - k, 0, 0))
    free, alias = chained(kept, 11)
    return pl.pallas_call(
        backward_kernel,
        out_shape=[shape(delta.shape, BF), shape(delta.shape), shape((docs, tokens // TB, 1, TB * n)),
                   shape((part, n, width)), shape((part, TB, width)), shape((part, n, width))],
        grid=(part, tokens // 2 // step),
        in_specs=[rows, rows, rows, rows, pl.BlockSpec((1, step * n, width), lambda g, k: (g + base, last - k, 0)),
                  pl.BlockSpec((1, nb, n, TB), lambda g, k: (g + base, last - k, 0, 0)),
                  pl.BlockSpec((1, nb, TB, TB * n), lambda g, k: (g + base, last - k, 0, 0)),
                  whole(rate.shape), state, whole(mask.shape), whole((1, width))] + free,
        out_specs=[rows, rows, line, state, pl.BlockSpec((1, TB, width), lambda g, k: (g, 0, 0)), state],
        scratch_shapes=[pltpu.VMEM((n, width), F32), pltpu.VMEM((2, TB * n, width), BF), pltpu.VMEM((2, TB * n, width), BF),
                        pltpu.VMEM((2, TB * n, 128), BF)],
        input_output_aliases=alias, compiler_params=params(), cost_estimate=cost(4), name="backward",
    )(pre, delta, mixed, dy, before, ct, bdiag, rate, qin, mask, skip, *kept)


def conv_back_kernel(dproj_ref, xproj_ref, dmix_ref, inner_ref, prev_ref, rim_ref, taps_ref, shift_ref, carry_ref, *refs,
                     lead, first):
    dinner_ref, tail_ref, head_ref, sums_ref, dm_ref, xs_ref, ds_ref = refs[-7:]
    step, width = dmix_ref.shape[1:]
    k = pl.program_id(1)

    @pl.when(k == 0)
    def _():
        ds_ref[step:] = carry_ref[0]
        sums_ref[0] = jnp.zeros(sums_ref.shape[1:], F32)

    dm_ref[...] = mm(dproj_ref[0], xproj_ref[...])
    xs_ref[:8] = jnp.where(k == pl.num_programs(1) - 1, rim_ref[0], prev_ref[0]) if first else prev_ref[0]
    xs_ref[8:] = inner_ref[0]
    cw = 256

    def tile(x):
        return jnp.sum(x.reshape(step // 8, 8, cw), axis=0)

    for c in range(0, width, cw):
        cs = pl.ds(c, cw)
        pre = shift_ref[:, cs]
        for tap in range(lead + 1):
            pre = pre + taps_ref[tap:tap + 1, cs] * xs_ref[pl.ds(8 - lead + tap, step), cs]
        sig = sigmoid(pre)
        d_conv = (dmix_ref[0, :, cs] + dm_ref[:, cs]) * (sig * (1.0 + pre * (1.0 - sig)))
        ds_ref[:step, cs] = d_conv
        sums_ref[0, :8, cs] += tile(d_conv)
        for tap in range(lead + 1):
            sums_ref[0, 8 + 8 * tap:16 + 8 * tap, cs] += tile(d_conv * xs_ref[pl.ds(8 - lead + tap, step), cs])
        back = taps_ref[lead:lead + 1, cs] * d_conv
        for m in range(1, lead + 1):
            back = back + taps_ref[lead - m:lead - m + 1, cs] * ds_ref[pl.ds(m, step), cs]
        dinner_ref[0, :, cs] = back.astype(BF)

        @pl.when(k == 0)
        def _():
            tail_ref[0, :, cs] = back[step - 8:]

        head_ref[0, :, cs] = d_conv[:8]
        ds_ref[step:, cs] = d_conv[:8]


def conv_back(begin, kept, carry, d_proj, xproj_t, d_mix, inner_x, rim, taps, shift, step=128):
    docs, tokens, width = d_mix.shape
    half = tokens // 2
    last = (begin + half) // step - 1
    count = half // step
    lead = taps.shape[0] - 1
    cols = xproj_t.shape[0]
    rows = pl.BlockSpec((1, step, width), lambda g, k: (g, last - k, 0))
    few = pl.BlockSpec((1, 8, width), lambda g, k: (g, 0, 0))
    sums = 8 * (lead + 2)
    free, alias = chained(kept, 9)
    return pl.pallas_call(
        functools.partial(conv_back_kernel, lead=lead, first=begin == 0),
        out_shape=[shape(d_mix.shape, BF), shape((docs, 8, width)), shape((docs, 8, width)), shape((docs, sums, width))],
        grid=(docs, count),
        in_specs=[pl.BlockSpec((1, step, cols), lambda g, k: (g, count - 1 - k, 0)), whole(xproj_t.shape), rows, rows,
                  pl.BlockSpec((1, 8, width), lambda g, k: (g, jnp.maximum((last - k) * (step // 8) - 1, 0), 0)), few,
                  whole(taps.shape), whole((1, width)), few] + free,
        out_specs=[rows, few, few, pl.BlockSpec((1, sums, width), lambda g, k: (g, 0, 0))],
        scratch_shapes=[pltpu.VMEM((step, width), F32), pltpu.VMEM((step + 8, width), F32), pltpu.VMEM((step + 8, width), F32)],
        input_output_aliases=alias, compiler_params=params(), cost_estimate=cost(0.2), name="conv_back",
    )(d_proj, xproj_t, d_mix, inner_x, inner_x, rim, taps, shift, carry, *kept)


def place_kernel(doc_ref, *refs, pieces):
    parts, (weight_ref, gain_ref, sum_ref) = refs[:pieces], refs[pieces:pieces + 3]
    out_ref, total_ref = refs[-2:]
    j = pl.program_id(0)

    def put(x):
        x = x.astype(F32)
        out_ref[...] = x * gain_ref[...]
        x = x * weight_ref[...].astype(F32)
        x = sum(x[:, c:c + 128] for c in range(0, x.shape[1], 128))
        total_ref[...] = jnp.where(j == 0, sum_ref[...], total_ref[...]) + x

    if pieces == 1:
        put(parts[0][...])
    else:
        for p in range(pieces):
            @pl.when(j == p)
            def _():
                put(parts[p][...])


def place(doc, kept, parts, weight, gain, sums, block, offset):
    rows, width = weight.shape
    docs = width // 2 // block
    at = (lambda j, doc_ref: (0, offset + j)) if len(parts) == 1 else (lambda j, doc_ref: (0, offset + (doc_ref[0] ^ j)))
    one = lambda j, doc_ref: (0, 0)
    piece_at = (lambda j, doc_ref: (0, j)) if len(parts) == 1 else one
    free = [pl.BlockSpec(memory_space=pl.ANY)] * len(kept)
    return pl.pallas_call(
        functools.partial(place_kernel, pieces=len(parts)),
        out_shape=[shape((rows, width)), shape((rows, 128))],
        grid_spec=pltpu.PrefetchScalarGridSpec(
            num_scalar_prefetch=1, grid=(docs,),
            in_specs=[pl.BlockSpec((rows, block), piece_at)] * len(parts)
            + [pl.BlockSpec((rows, block), at), pl.BlockSpec((rows, 1), one), pl.BlockSpec((rows, 128), one)] + free,
            out_specs=[pl.BlockSpec((rows, block), at), pl.BlockSpec((rows, 128), one)]),
        input_output_aliases={4 + len(parts): 0} if kept else {},
        compiler_params=params(), cost_estimate=cost(0.1), name="place",
    )(doc, *parts, weight, gain, sums, *kept)


def input_kernel(part_ref, one_ref, two_ref, hidden_ref, cot_ref, out_ref):
    d_normed = part_ref[...] + one_ref[...].astype(F32) + two_ref[...].astype(F32)
    r = hidden_ref[...].astype(F32)
    scale = lax.rsqrt(jnp.mean(r * r, axis=1, keepdims=True) + NORM_EPS)
    scaled = r * scale
    out_ref[...] = cot_ref[...].astype(F32) + scale * (d_normed - scaled * jnp.mean(d_normed * scaled, axis=1, keepdims=True))


def input_gradient(part, one, two, hidden, cot, step=128):
    rows = pl.BlockSpec((step, hidden.shape[1]), lambda k: (k, 0))
    return pl.pallas_call(
        input_kernel, out_shape=shape(hidden.shape), grid=(hidden.shape[0] // step,),
        in_specs=[rows] * 5, out_specs=rows, compiler_params=params(), cost_estimate=cost(0.1), name="input_gradient",
    )(part, one, two, hidden, cot)


def shifted(block, axis, distance):
    devices = range(lax.axis_size(axis))
    route = [(i - distance, i) for i in devices if i - distance in devices]
    return lax.ppermute(block, axis, route)


def swap(x, axis, flip):
    return lax.ppermute(x, axis, [(i, i ^ flip) for i in range(lax.axis_size(axis))])


def piece(x, index, size, axis):
    return lax.dynamic_slice_in_dim(x, index * size, size, axis)


def chain(decays, states, order, keep, start):
    state = start
    for k in order:
        decay = decays[k].astype(F32)
        state = jnp.where(keep(k), decay * state + states[k].astype(F32), state)
    return state


def doc_gather(x):
    return [x] + [swap(x, "doc", j) for j in (1, 2, 3)]


def doc_sum(parts):
    total = parts[0].astype(F32)
    for j in (1, 2, 3):
        total = total + swap(parts[j].astype(BF), "doc", j).astype(F32)
    return total


def doc_place(parts, doc, axis):
    stack = jnp.stack(parts)
    return jnp.concatenate([lax.dynamic_index_in_dim(stack, doc ^ k, 0, False) for k in range(len(parts))], axis=axis)


def shards(hidden_in, cotangent, scan_init, conv_init, norm_gain, in_weight, conv_weight, conv_bias,
           xproj_weight, dt_weight, dt_bias, a_log, skip_d, out_weight):
    docs, seqs = lax.axis_size("doc"), lax.axis_size("seq")
    doc, seq = lax.axis_index("doc"), lax.axis_index("seq")
    near = seqs == 2 * docs == 8
    hidden, cot = hidden_in[0], cotangent[0]
    tokens, width = hidden.shape
    inner = in_weight.shape[1] // 2
    rank = dt_weight.shape[0]
    states = a_log.shape[0]
    lead = conv_init.shape[1]
    taps = conv_weight.shape[0]
    block = inner // docs
    rows_all = docs * tokens
    blocks = tokens // TB
    middle = tokens // 2
    slots = range(docs)

    def mine(x, offset=0):
        return lax.dynamic_slice_in_dim(x, offset + doc * block, block, x.ndim - 1)

    def mine_of(x, owner):
        return piece(x, owner, block, 1)

    def seq_gather(x):
        return lax.all_gather(x, "seq", axis=0, tiled=True)

    state_rows, lead_rows = states * block // width, 2 * (-(-lead * block // (2 * width)))

    def first_of(j):
        rows = mine_of(conv_init[0], doc ^ j)
        rows = jnp.pad(rows, ((0, lead_rows * width // block - lead), (0, 0))).reshape(lead_rows, width)
        start = mine_of(scan_init[0], doc ^ j).astype(BF).reshape(state_rows, width)
        packed = jnp.concatenate([hidden[tokens - 16:], start, rows], axis=0)
        return jnp.pad(packed, ((0, 32 - packed.shape[0]), (0, 0)))

    halo = [lax.ppermute(first_of(j), ("doc", "seq"),
                         [(d * seqs + s, (d ^ j) * seqs + (s + 1) % seqs) for d in slots for s in range(seqs)])
            for j in slots]
    top, low = hidden[:middle], tie(hidden[middle:], *halo)
    one, two = ([swap(x, "doc", j) for x in (top, low)] for j in (1, 2))
    scaled_weight = (in_weight.astype(F32) * norm_gain.astype(F32)[:, None]).astype(BF)
    w_inner = seq_gather(mine(scaled_weight))
    few = jnp.concatenate([conv_weight, conv_bias[None], dt_bias[None], skip_d[None]], axis=0)
    few = jnp.pad(few, ((0, 16 - few.shape[0]), (0, 0)))
    small = jnp.concatenate([few, a_log, dt_weight, xproj_weight.T], axis=0)
    if near:
        route = [((d, 2 * z + c), (z, 2 * d + c)) for d in slots for z in slots for c in range(2)]
        turn = [(a * seqs + b, e * seqs + f) for (a, b), (e, f) in route]
        half = lax.ppermute(small, ("doc", "seq"), turn)
        half = tie(half, *one, *two)
        other = swap(half, "seq", 1)
        core = seq % 2 == 0
        small = jnp.concatenate([jnp.where(core, half, other), jnp.where(core, other, half)], axis=1)
    else:
        small = mine(lax.all_gather(small, "seq", axis=1, tiled=True))
    three = [swap(two[0], "doc", 1), swap(one[1], "doc", 2)]
    w_gate = seq_gather(tie(mine(scaled_weight, inner), small))
    w_out = seq_gather(mine(out_weight))

    wide = small.astype(F32)
    conv_taps, conv_shift, dt_shift, skip = wide[:taps], wide[taps][None], wide[taps + 1][None], wide[taps + 2][None]
    at = 16
    rate = -jnp.exp(wide[at:at + states])
    dt_full = small[at + states:at + states + rank]
    xproj_t = small[at + states + rank:]
    rate2 = rate * (1.0 / LN2)

    is_first = (seq == 0).astype(jnp.int32)[None]

    def first_rows(x):
        rows = x[16 + state_rows:16 + state_rows + lead_rows].reshape(-1, block)[:lead].astype(F32)
        return jnp.pad(rows, ((8 - lead, 0), (0, 0)))

    kept, proj_part = (), []
    for j, x in enumerate(((top, low), one, two, three)):
        if j == 3:
            x = [tie(half, kept[0]) for half in three]
            cot_top = tie(cot[:middle], *x)
            cot_near = [swap(cot_top, "doc", 1), swap(cot_top, "doc", 2)]
        *kept, part = front(j, docs, kept, is_first, *x, halo[j], w_inner, small, lead,
                            rank + 2 * states, first_rows(halo[j]))
        proj_part.append(part)
    normed, inner_x, mixed, rim = kept
    mixed_flat = mixed.reshape(rows_all, block)

    w_gate = tie(w_gate, *proj_part)
    gate_in = mm(normed, w_gate)
    got = [tie(swap(proj_part[j].astype(BF), "doc", j), gate_in) for j in slots[1:]]
    proj_own = (proj_part[0] + sum(x.astype(F32) for x in got)).astype(BF)
    proj = jnp.concatenate(doc_gather(proj_own), axis=0)
    proj = tie(proj, *cot_near)
    cot_low = tie(cot[middle:], proj)
    cot_rest = [swap(cot_low, "doc", 1), swap(cot_low, "doc", 2)]
    cot_far = [swap(tie(cot_near[1], proj), "doc", 1)]
    init = jnp.stack([x[16:16 + state_rows].reshape(states, block) for x in halo]).astype(F32)
    rank_in = proj[:, :rank]
    gate_in = gate_in.reshape(docs, tokens, block)

    mask = jnp.repeat(jnp.eye(TB, dtype=F32), states, axis=1)
    spread = jnp.tile(jnp.eye(states, dtype=BF), (1, TB))

    def columns(x):
        return jnp.swapaxes(x.reshape(docs, blocks, TB, states), 2, 3).astype(F32)

    def diagonal(x):
        return (mm(x, spread).reshape(docs, blocks, TB, TB * states) * mask).astype(BF)

    b_rows, c_rows = proj[:, rank:rank + states], proj[:, rank + states:]
    b_cols, c_cols = columns(b_rows), columns(c_rows)
    b_diag, c_diag = diagonal(b_rows), diagonal(c_rows)

    rank_in = rank_in.reshape(docs, tokens, rank)
    part = docs // 2
    starts, decays = {}, {}
    kept = ()
    for base in (part, 0):
        *kept, end_state, decay = summary(base, part, kept, rank_in, dt_full, dt_shift, mixed, b_cols, rate2)
        if base == 0:
            end_state = tie(end_state, *cot_far)
        ends = lax.all_gather(jnp.stack([end_state, decay]).astype(BF), "seq")
        decays[base] = ends[:, 1]
        starts[base] = chain(ends[:, 1], ends[:, 0], range(seqs), lambda k: k < seq, init[base:base + part])
        if base:
            cot_far.append(swap(tie(cot_rest[0], end_state), "doc", 2))
            kept[0] = tie(kept[0], cot_rest[0], w_out)
    dt_pre, delta = kept
    rank_in = rank_in.reshape(rows_all, rank)

    cot_all = jnp.concatenate([cot_top, cot_low, cot_near[0], cot_rest[0], cot_near[1], cot_rest[1], *cot_far], axis=0)
    cot_all = tie(cot_all, end_state)
    def relay_far(x):
        x, half = x.astype(BF), x.shape[0] // 32 * 16
        return swap(x[:half], "doc", 1), swap(x[half:], "doc", 2)

    def relay_near(parts, one, two):
        half = one.shape[0]
        first = jnp.concatenate([parts[1][:half], parts[1][half:] + two.astype(F32)], axis=0).astype(BF)
        second = jnp.concatenate([parts[2][:half] + one.astype(F32), parts[2][half:]], axis=0).astype(BF)
        return first, second

    d_start, skip_grad, out_rows = {}, [], {}
    kept = ()
    for base in (part, 0):
        rows = slice(base * tokens, (base + part) * tokens)
        d_gated = mm(cot_all[rows], w_out).reshape(part, tokens, block)
        if base == 0:
            d_gated = tie(d_gated, *out_rows.values())
        *kept, d_start[base], skip_part = forward(base, part, kept, delta, mixed, gate_in, d_gated, b_cols, c_diag, rate2,
                                                  starts[base], mask, skip)
        skip_grad.append(skip_part)
        for j in range(base + part - 1, base - 1, -1):
            out_rows[j] = mm_last(kept[2][j], w_out)
        if base:
            out_far = relay_far(out_rows[3])
    out_far = [tie(x, d_start[0]) for x in out_far]
    d_y, before, gated, d_gate, d_out = kept
    gated, d_gate = gated.reshape(rows_all, block), d_gate.reshape(rows_all, block)
    skip_grad = sum(jnp.sum(x, axis=(0, 1)) for x in skip_grad)
    later = lax.all_gather(jnp.concatenate([d_start[0], d_start[part]], axis=0).astype(BF), "seq")
    decays = jnp.concatenate([decays[0], decays[part]], axis=1)
    zero = jnp.zeros((docs, states, block), F32)
    back = range(seqs - 1, -1, -1)
    later_sum = chain(decays, later, back, lambda k: k > seq, zero)
    first_sum = chain(decays, later, back, lambda k: True, zero)

    def seq_sum(x):
        return lax.psum_scatter(x, "seq", scatter_dimension=0, tiled=True)

    def all_blocks(total):
        return lax.all_gather(total, "doc", axis=1, tiled=True)

    out_first, out_second = relay_near(out_rows, *out_far)
    out_got = swap(out_first, "doc", 1), swap(out_second, "doc", 2)
    gated = tie(gated, out_first, out_second)
    out_part = mm_first(cot_all, gated).astype(BF)
    gate_part = mm_first(normed, d_gate).astype(BF)
    later_sum = tie(later_sum, out_part, gate_part)
    out_part, gate_part = seq_sum(out_part), seq_sum(gate_part)

    d_out = d_out.reshape(docs, tokens, states)

    def proj_parts(kept, begin):
        rows = slice(begin, begin + middle)
        d_rank = mm_last(kept[0][:, rows].reshape(docs * middle, block), dt_full).reshape(docs, middle, rank)
        d_in = kept[2].reshape(docs, tokens, states)[:, rows]
        full = jnp.concatenate([d_rank, d_in, d_out[:, rows]], axis=2)
        return full[0], [full[j].astype(BF) for j in slots[1:]]

    def run_back(begin, kept, state):
        return backward(0, docs, begin, kept, dt_pre, delta, mixed, d_y, before, c_cols, b_diag, rate2, state, mask, skip)

    *kept, rate_grad, dt_bias_grad, passed_on = run_back(middle, (), later_sum)
    kept[0] = tie(kept[0], *out_got)
    out_got = [tie(x, kept[2]) for x in out_got]
    out_total = all_blocks(tie(out_part, kept[2]))
    own_late, sent = proj_parts(kept, middle)
    got = [swap(x, "doc", j) for j, x in zip(slots[1:], sent)]
    kept[0] = tie(kept[0], *sent)
    *kept, rate_part, bias_part, _ = run_back(0, kept, passed_on)
    got = [tie(x, kept[2]) for x in got]
    own_late = (own_late + sum(x.astype(F32) for x in got)).astype(BF)
    kept[0] = tie(kept[0], own_late, out_total)
    gate_total = all_blocks(tie(gate_part, kept[2]))
    late = [own_late] + [swap(own_late, "doc", j) for j in slots[1:]]
    d_pre, d_mix, _ = kept
    rate_grad = jnp.sum(rate_grad + rate_part, axis=0)
    dt_bias_grad = jnp.sum(dt_bias_grad + bias_part, axis=(0, 1))
    own_early, sent = proj_parts(kept, 0)
    got = [swap(x, "doc", j) for j, x in zip(slots[1:], sent)]

    nothing = jnp.zeros((docs, 8, block), F32)
    d_proj_late = tie(jnp.stack(late), *sent)
    d_inner, tail, carry, sums_late = conv_back(middle, (), nothing, d_proj_late, xproj_t, d_mix, inner_x, rim, conv_taps,
                                                conv_shift)
    d_gate = tie(d_gate, *sent).reshape(docs, tokens, block)
    gate_far = mm_last(d_gate[3], w_gate)
    own_early = (own_early + sum(x.astype(F32) for x in got)).astype(BF)
    d_inner = tie(d_inner, own_early)
    early = [own_early] + [swap(own_early, "doc", j) for j in slots[1:]]

    d_inner = tie(d_inner, gate_far, *early[1:])
    d_proj_early = jnp.stack(early)
    d_proj = jnp.concatenate([d_proj_early, d_proj_late], axis=1).reshape(rows_all, -1)
    few = jnp.concatenate([rate_grad, dt_bias_grad[None], skip_grad[None], jnp.zeros((14, block), F32)], axis=0)
    small_grad = [few, mm_first(rank_in, d_pre.reshape(rows_all, block)),
                  mm_first(d_proj, mixed_flat)]
    if near:
        side = seq % 2
        small_sum, sent = (jnp.concatenate([piece(x, at_side, block // 2, 1) for x in small_grad], axis=0)
                           for at_side in (side, 1 - side))
        small_sum = (small_sum + swap(sent.astype(BF), "seq", 1).astype(F32)).astype(BF)
        turned = lax.ppermute(small_sum, ("doc", "seq"), turn)
        d_proj_early = tie(d_proj_early, small_sum, gate_total)
    else:
        small_grad = jnp.concatenate(small_grad, axis=0)
        small_sum = lax.psum_scatter(small_grad, "seq", scatter_dimension=1, tiled=True)
        small_sum = lax.all_gather(small_sum.astype(BF), ("doc", "seq"), axis=1, tiled=True)
        turned = piece(small_sum, seq, inner // seqs, 1).astype(F32)

    d_inner, _, head, sums = conv_back(0, [d_inner], carry, d_proj_early, xproj_t, d_mix, inner_x, rim, conv_taps, conv_shift)
    d_ext = jnp.stack([sum(conv_taps[k] * head[:, j - k] for k in range(j + 1)) for j in range(lead)], axis=1)
    passed = shifted(d_ext.astype(BF), "seq", -1).astype(F32)
    d_inner = lax.dynamic_update_slice(d_inner, (tail[:, 8 - lead:] + passed).astype(BF), (0, tokens - lead, 0))
    d_inner = tie(d_inner, turned)
    inner_part = mm_first(normed, d_inner.reshape(rows_all, block)).astype(BF)
    d_inner = tie(d_inner, inner_part)
    inner_part = seq_sum(inner_part)
    small_sum = sum(x.astype(F32) for x in doc_gather(turned)) if near else turned
    d_inner = tie(d_inner, small_sum)

    d_gate = tie(d_gate, d_inner)

    def normed_part(j):
        return mm_last(d_inner[j], w_inner) + mm_last(d_gate[j], w_gate)

    far = mm_last(d_inner[3], w_inner) + gate_far
    far_got = relay_far(far)
    d_inner = tie(d_inner, far)
    parts = [normed_part(j) for j in range(3)]
    first, second = relay_near(parts, *(tie(x, parts[0]) for x in far_got))
    early_got = swap(first, "doc", 1), swap(second, "doc", 2)
    inner_total = all_blocks(tie(inner_part, first, second))
    gain = norm_gain.astype(F32)[:, None]
    in_total, gain_sum = place(doc[None], [], [gate_total], in_weight, gain, jnp.zeros((width // seqs, 128), F32), block, docs)

    output = (hidden.astype(F32) + out_rows[0] + sum(x.astype(F32) for x in out_got)).astype(BF)
    sums = jnp.sum((sums + sums_late).reshape(docs, taps + 1, 8, block), axis=(0, 2))
    ends = jnp.concatenate([jnp.where(seq == 0, tie(d_ext, *early_got, inner_part), 0.0).reshape(docs * lead, block), sums], axis=0)
    if near:
        for flip in (1, 2, 4):
            ends = ends + swap(ends, "seq", flip)
    else:
        ends = lax.psum(ends, "seq")
    sends = [jnp.concatenate([first_sum[j], ends[j * lead:(j + 1) * lead], ends[docs * lead:]], axis=0) for j in slots]
    ends = doc_place([sends[0]] + [swap(sends[j], "doc", j) for j in slots[1:]], doc, 1)
    init_grad, conv_sum = ends[:states + lead], piece(ends[states + lead:], seq, inner // seqs, 1)
    input_grad = input_gradient(parts[0], *early_got, hidden, cot)
    in_total, gain_sum = place(doc[None], [in_total], [inner_total], in_weight, gain, gain_sum, block, 0)
    gain_sum = jnp.sum(gain_sum, axis=1)

    return (
        output[None],
        input_grad[None],
        init_grad[None, :states],
        init_grad[None, states:],
        gain_sum,
        in_total,
        conv_sum[1:],
        conv_sum[0],
        small_sum[states + 16 + rank:].T,
        small_sum[states + 16:states + 16 + rank],
        small_sum[states],
        small_sum[:states],
        small_sum[states + 1],
        out_total.astype(F32),
    )


def solution(mesh):
    placed = (
        P("doc", "seq", None), P("doc", "seq", None), P("doc", None, None), P("doc", None, None),
        P("seq"), P("seq", None), P(None, "seq"), P("seq"), P("seq", None), P(None, "seq"),
        P("seq"), P(None, "seq"), P("seq"), P("seq", None),
    )
    return jax.shard_map(shards, mesh=mesh, in_specs=placed, out_specs=placed, check_vma=False)
```

```python
import functools
import jax
import jax.numpy as jnp
from jax import lax
from jax.experimental import pallas as pl
from jax.experimental.pallas import tpu as pltpu
from jax.sharding import PartitionSpec as P

TB = 16
F32 = jnp.float32
BF = jnp.bfloat16
LN2 = 0.6931471805599453
NORM_EPS = 1e-05
LAST = (((1,), (1,)), ((), ()))
FIRST = (((0,), (0,)), ((), ()))


def mm(a, b):
    return jnp.dot(a, b, preferred_element_type=F32)


def mm_last(a, b):
    return lax.dot_general(a, b, LAST, preferred_element_type=F32)


def mm_first(a, b):
    return lax.dot_general(a, b, FIRST, preferred_element_type=F32)


def cost(us):
    return pl.CostEstimate(flops=int(us * 1.0e9), bytes_accessed=0, transcendentals=0)


def params():
    return pltpu.CompilerParams(vmem_limit_bytes=56 * 2**20)


def shape(dims, kind=F32):
    return jax.ShapeDtypeStruct(dims, kind)


def whole(dims):
    return pl.BlockSpec(dims, lambda *_: (0,) * len(dims))


def tie(x, *tokens):
    free = pl.BlockSpec(memory_space=pl.ANY)
    return pl.pallas_call(lambda *refs: None, out_shape=shape(x.shape, x.dtype),
                          in_specs=[free] * (1 + len(tokens)), out_specs=free, input_output_aliases={0: 0},
                          name="tie")(x, *tokens)


def sigmoid(x):
    return 0.5 + 0.5 * jnp.tanh(0.5 * x)


def tiles(x):
    return sum(x[:, c:c + 128] for c in range(0, x.shape[1], 128))


def softplus(x):
    return jnp.maximum(x, 0.0) + jnp.log1p(jnp.exp(-jnp.abs(x)))


def front_kernel(first_ref, top_ref, low_ref, halo_ref, w_ref, few_ref, xproj_ref, init_ref, *refs, lead):
    taps, shift = few_ref[:lead + 1].astype(F32), few_ref[lead + 1:lead + 2].astype(F32)
    normed_ref, inner_ref, mixed_ref, rim_ref, proj_ref, xs_ref = refs[-6:]
    step, width = top_ref.shape[0], xs_ref.shape[1]

    def normalise(x):
        r = x.astype(F32)
        scale = lax.rsqrt(jnp.mean(r * r, axis=1, keepdims=True) + NORM_EPS)
        return (r * scale).astype(BF)

    @pl.when(pl.program_id(0) == 0)
    def _():
        before = mm(normalise(halo_ref[...]), w_ref[...])[halo_ref.shape[0] - 8:]
        rim = jnp.where(first_ref[0] == 1, init_ref[...], before)
        rim_ref[0] = rim
        xs_ref[:8] = rim

    in_top = 2 * pl.program_id(0) < pl.num_programs(0)
    normed_ref[...] = normalise(jnp.where(in_top, top_ref[...], low_ref[...]))
    x = mm(normed_ref[...], w_ref[...])
    inner_ref[0] = x
    xs_ref[8:] = x
    for c in range(0, width, 256):
        cs = pl.ds(c, 256)
        pre = shift[:, c:c + 256]
        for tap in range(lead + 1):
            pre = pre + taps[tap:tap + 1, c:c + 256] * xs_ref[pl.ds(8 - lead + tap, step), cs]
        mixed_ref[0, :, cs] = (pre * sigmoid(pre)).astype(BF)
    proj_ref[...] = mm_last(mixed_ref[0], xproj_ref[...])
    xs_ref[:8] = xs_ref[step:step + 8]


def front(slot, docs, kept, first, top, low, halo, w, small, lead, cols, init, step=256):
    width, block = w.shape
    extra = 16
    tokens = 2 * top.shape[0]
    count = tokens // step
    rows = pl.BlockSpec((1, step, block), lambda k: (slot, k, 0))
    few = pl.BlockSpec((1, 8, block), lambda k: (slot, 0, 0))
    return pl.pallas_call(
        functools.partial(front_kernel, lead=lead),
        out_shape=[shape((docs * tokens, width), BF), shape((docs, tokens, block)), shape((docs, tokens, block), BF),
                   shape((docs, 8, block)), shape((tokens, cols))],
        grid=(count,),
        in_specs=[pl.BlockSpec(memory_space=pltpu.SMEM), pl.BlockSpec((step, width), lambda k: (jnp.minimum(k, count // 2 - 1), 0)),
                  pl.BlockSpec((step, width), lambda k: (jnp.maximum(k - count // 2, 0), 0)),
                  pl.BlockSpec((extra, width), lambda k: (0, 0)), whole(w.shape),
                  whole((16, block)), pl.BlockSpec((cols, block), lambda k: (1, 0)), whole((8, block))]
        + [pl.BlockSpec(memory_space=pl.ANY)] * len(kept),
        out_specs=[pl.BlockSpec((step, width), lambda k: (slot * count + k, 0)), rows, rows, few,
                   pl.BlockSpec((step, cols), lambda k: (k, 0))],
        scratch_shapes=[pltpu.VMEM((step + 8, block), F32)],
        input_output_aliases={8 + i: i for i in range(len(kept))},
        compiler_params=params(), cost_estimate=cost(0.1), name="front",
    )(first, top, low, halo, w, small, small, init, *kept)


def summary_kernel(rank_ref, dtw_ref, shift_ref, mixed_ref, bt_ref, rate_ref, *refs):
    pre_ref, delta_ref, end_ref, decay_ref = refs[-4:]
    tokens, width = mixed_ref.shape[1:]
    rate = rate_ref[...]
    group = 4
    count = tokens // (TB * group)

    def steps(i):
        rows = pl.ds(pl.multiple_of(i * TB * group, TB * group), TB * group)
        pre = mm(rank_ref[0, rows], dtw_ref[...]) + shift_ref[...]
        pre_ref[0, rows] = pre
        delta_ref[0, rows] = softplus(pre)

    steps(0)

    def body(i, carry):
        h, total = carry
        for b in range(group):
            rows = pl.ds(pl.multiple_of((i * group + b) * TB, TB), TB)
            dl = delta_ref[0, rows]
            dr = dl * mixed_ref[0, rows].astype(F32)
            bt = bt_ref[0, i * group + b]
            for t in range(TB):
                h = jnp.exp2(dl[t:t + 1] * rate) * h + bt[:, t:t + 1] * dr[t:t + 1]
            total = total + dl
        steps(jnp.minimum(i + 1, count - 1))
        return h, total

    h, total = lax.fori_loop(0, count, body, (jnp.zeros(rate.shape, F32), jnp.zeros((TB, width), F32)))
    end_ref[0] = h
    decay_ref[0] = jnp.exp2(jnp.sum(total, axis=0, keepdims=True) * rate)


def chained(kept, before):
    return [pl.BlockSpec(memory_space=pl.ANY)] * len(kept), {before + i: i for i in range(len(kept))}


def summary(base, count, kept, rank_in, dtw, shift, mixed, bt, rate):
    docs, tokens, width = mixed.shape
    n, rank = rate.shape[0], rank_in.shape[2]
    rows = pl.BlockSpec((1, tokens, width), lambda g: (g + base, 0, 0))
    state = pl.BlockSpec((1, n, width), lambda g: (g, 0, 0))
    free, alias = chained(kept, 6)
    return pl.pallas_call(
        summary_kernel,
        out_shape=[shape((docs, tokens, width))] * 2 + [shape((count, n, width))] * 2,
        grid=(count,),
        in_specs=[pl.BlockSpec((1, tokens, rank), lambda g: (g + base, 0, 0)), whole(dtw.shape), whole((1, width)), rows,
                  pl.BlockSpec((1, tokens // TB, n, TB), lambda g: (g + base, 0, 0, 0)), whole(rate.shape)] + free,
        out_specs=[rows, rows, state, state], input_output_aliases=alias,
        compiler_params=params(), cost_estimate=cost(22), name="summary",
    )(rank_in, dtw, shift, mixed, bt, rate, *kept)


def forward_kernel(delta_ref, mixed_ref, gate_ref, dg_ref, bt_ref, cdiag_ref, rate_ref, start_ref, mask_ref, skip_ref,
                   *refs):
    dy_ref, before_ref, gated_ref, dgate_ref, dout_ref, dstart_ref, sgrad_ref, hs_ref, ps_ref, hb_ref, zb_ref, sb_ref, sig_ref = refs[-13:]
    tokens = delta_ref.shape[1]
    n = rate_ref.shape[0]
    count = tokens // TB
    rate = rate_ref[...]

    @pl.when(pl.program_id(1) == 0)
    def _():
        hs_ref[...] = start_ref[0]
        ps_ref[...] = jnp.ones_like(ps_ref)
        dstart_ref[0] = jnp.zeros(dstart_ref.shape[1:], F32)
        sgrad_ref[0] = jnp.zeros(sgrad_ref.shape[1:], F32)

    mask = mask_ref[...]
    spread = lax.rem(lax.broadcasted_iota(jnp.int32, mask.shape, 1), n) == lax.broadcasted_iota(jnp.int32, mask.shape, 0)

    def finish(i, hm, good):
        rows = pl.ds(pl.multiple_of(i * TB, TB), TB)
        gate, dg, sig = gate_ref[0, rows], dg_ref[0, rows], sig_ref[...]
        act = gate * sig
        mx = mixed_ref[0, rows].astype(F32)
        y = mm(cdiag_ref[0, i], hm) + skip_ref[...] * mx
        gated_ref[0, rows] = (y * act).astype(BF)
        dgate_ref[0, rows] = (dg * y * (sig * (1.0 + gate * (1.0 - sig)))).astype(BF)
        dout_ref[0, i] = mm_last(jnp.ones((8, 128), BF), sb_ref[...])[:1]
        weight = jnp.where(spread, jnp.sum(cdiag_ref[0, i].astype(F32), axis=0, keepdims=True), 0.0).astype(BF)
        dstart_ref[0] += jnp.where(good, mm(weight, zb_ref[...]), 0.0)

    def body(i, carry):
        h, p = carry
        rows = pl.ds(pl.multiple_of(i * TB, TB), TB)
        dl = delta_ref[0, rows]
        mx = mixed_ref[0, rows].astype(F32)
        dr = dl * mx
        gate = gate_ref[0, rows]
        sig = sigmoid(gate)
        dy = dg_ref[0, rows] * (gate * sig)
        dy_ref[0, rows] = dy
        sgrad_ref[0] += dy * mx
        bt = bt_ref[0, i]
        hb = h.astype(BF)
        before_ref[0, pl.ds(pl.multiple_of(i * TB * n, TB * n), n)] = hb
        last = jnp.maximum(i - 1, 0)
        finish(last, before_ref[0, pl.ds(pl.multiple_of((last * TB + 1) * n, n), TB * n)], i > 0)
        sig_ref[...] = sig
        for t in range(TB):
            if t:
                before_ref[0, pl.ds(pl.multiple_of((i * TB + t) * n, n), n)] = hb
            a = jnp.exp2(dl[t:t + 1] * rate)
            h = a * h + bt[:, t:t + 1] * dr[t:t + 1]
            hb = h.astype(BF)
            sb_ref[t * n:(t + 1) * n] = tiles(h * dy[t:t + 1]).astype(BF)
            p = p * a
            zb_ref[t * n:(t + 1) * n] = (p * dy[t:t + 1]).astype(BF)
        return h, p

    h, p = lax.fori_loop(0, count, body, (hs_ref[...], ps_ref[...]))
    hs_ref[...] = h
    ps_ref[...] = p
    hb_ref[:(TB - 1) * n] = before_ref[0, ((count - 1) * TB + 1) * n:count * TB * n]
    hb_ref[(TB - 1) * n:] = h.astype(BF)
    finish(count - 1, hb_ref[...], True)


def forward(base, part, kept, delta, mixed, gate, d_gated, bt, cdiag, rate, start, mask, skip, step=128):
    docs, tokens, width = delta.shape
    n, nb = rate.shape[0], step // TB
    rows = pl.BlockSpec((1, step, width), lambda g, k: (g + base, k, 0))
    own = pl.BlockSpec((1, step, width), lambda g, k: (g, k, 0))
    state = pl.BlockSpec((1, n, width), lambda g, k: (g, 0, 0))
    cols = pl.BlockSpec((1, nb, n, TB), lambda g, k: (g + base, k, 0, 0))
    free, alias = chained(kept, 10)
    return pl.pallas_call(
        forward_kernel,
        out_shape=[shape(delta.shape), shape((docs, tokens * n, width), BF), shape(delta.shape, BF), shape(delta.shape, BF),
                   shape((docs, tokens // TB, 1, TB * n)), shape((part, n, width)), shape((part, TB, width))],
        grid=(part, tokens // step),
        in_specs=[rows, rows, rows, own, cols, pl.BlockSpec((1, nb, TB, TB * n), lambda g, k: (g + base, k, 0, 0)),
                  whole(rate.shape), state, whole(mask.shape), whole((1, width))] + free,
        out_specs=[rows, pl.BlockSpec((1, step * n, width), lambda g, k: (g + base, k, 0)), rows, rows,
                   pl.BlockSpec((1, nb, 1, TB * n), lambda g, k: (g + base, k, 0, 0)), state,
                   pl.BlockSpec((1, TB, width), lambda g, k: (g, 0, 0))],
        scratch_shapes=[pltpu.VMEM((n, width), F32), pltpu.VMEM((n, width), F32), pltpu.VMEM((TB * n, width), BF),
                        pltpu.VMEM((TB * n, width), BF), pltpu.VMEM((TB * n, 128), BF), pltpu.VMEM((TB, width), F32)],
        input_output_aliases=alias, compiler_params=params(), cost_estimate=cost(45), name="forward",
    )(delta, mixed, gate, d_gated, bt, cdiag, rate, start, mask, skip, *kept)


def backward_kernel(pre_ref, delta_ref, mixed_ref, dy_ref, before_ref, ct_ref, bdiag_ref, rate_ref, qin_ref, mask_ref, skip_ref,
                    *refs):
    dpre_ref, dmix_ref, din_ref, drate_ref, bgrad_ref, qout_ref, ps_ref, qb_ref, wb_ref, sb_ref = refs[-10:]
    tokens = delta_ref.shape[1]
    n = rate_ref.shape[0]
    count = tokens // TB
    rate = rate_ref[...]

    @pl.when(pl.program_id(1) == 0)
    def _():
        ps_ref[...] = qin_ref[0]
        drate_ref[0] = jnp.zeros(drate_ref.shape[1:], F32)
        bgrad_ref[0] = jnp.zeros(bgrad_ref.shape[1:], F32)

    mask = mask_ref[...]
    spread = lax.rem(lax.broadcasted_iota(jnp.int32, mask.shape, 1), n) == lax.broadcasted_iota(jnp.int32, mask.shape, 0)
    sums = jnp.concatenate([mask, spread.astype(F32)], axis=0).astype(BF)

    fold = jnp.ones((8, 128), BF)

    def finish(i, good, side):
        rows = pl.ds(pl.multiple_of(i * TB, TB), TB)
        dl = delta_ref[0, rows]
        mx = mixed_ref[0, rows].astype(F32)
        d_drive = mm(bdiag_ref[0, i], qb_ref[side])
        both = LN2 * mm(sums, wb_ref[side])
        din_ref[0, i] = mm_last(fold, sb_ref[side])[:1]
        drate_ref[0] += jnp.where(good, both[TB:], 0.0)
        sig = sigmoid(pre_ref[0, rows])
        d_pre = both[:TB] * jnp.where(dl > 1e-30, sig / dl, 1.0) + mx * d_drive * sig
        dpre_ref[0, rows] = d_pre.astype(BF)
        bgrad_ref[0] += jnp.where(good, d_pre, 0.0)
        dmix_ref[0, rows] = dl * d_drive + dy_ref[0, rows] * skip_ref[...]

    def scan(i, p, side):
        rows = pl.ds(pl.multiple_of(i * TB, TB), TB)
        dl = delta_ref[0, rows]
        dr = dl * mixed_ref[0, rows].astype(F32)
        dy = dy_ref[0, rows]
        ct = ct_ref[0, i]
        for t in reversed(range(TB)):
            q = ct[:, t:t + 1] * dy[t:t + 1] + p
            qb_ref[side, t * n:(t + 1) * n] = q.astype(BF)
            sb_ref[side, t * n:(t + 1) * n] = tiles(q * dr[t:t + 1]).astype(BF)
            x = dl[t:t + 1] * rate
            p = jnp.exp2(x) * q
            e = p * before_ref[0, pl.ds(pl.multiple_of((i * TB + t) * n, n), n)].astype(F32)
            wb_ref[side, t * n:(t + 1) * n] = (x * e).astype(BF)
        return p

    def body(j, p):
        i = count - 1 - 2 * j
        finish(jnp.minimum(i + 1, count - 1), j > 0, 1)
        p = scan(i, p, 0)
        finish(i, True, 0)
        return scan(i - 1, p, 1)

    ps_ref[...] = lax.fori_loop(0, count // 2, body, ps_ref[...])
    finish(0, True, 1)
    qout_ref[0] = ps_ref[...]


def backward(base, part, begin, kept, pre, delta, mixed, dy, before, ct, bdiag, rate, qin, mask, skip, step=128):
    docs, tokens, width = delta.shape
    n, nb, last = rate.shape[0], step // TB, (begin + tokens // 2) // step - 1
    rows = pl.BlockSpec((1, step, width), lambda g, k: (g + base, last - k, 0))
    state = pl.BlockSpec((1, n, width), lambda g, k: (g, 0, 0))
    line = pl.BlockSpec((1, nb, 1, TB * n), lambda g, k: (g + base, last - k, 0, 0))
    free, alias = chained(kept, 11)
    return pl.pallas_call(
        backward_kernel,
        out_shape=[shape(delta.shape, BF), shape(delta.shape), shape((docs, tokens // TB, 1, TB * n)),
                   shape((part, n, width)), shape((part, TB, width)), shape((part, n, width))],
        grid=(part, tokens // 2 // step),
        in_specs=[rows, rows, rows, rows, pl.BlockSpec((1, step * n, width), lambda g, k: (g + base, last - k, 0)),
                  pl.BlockSpec((1, nb, n, TB), lambda g, k: (g + base, last - k, 0, 0)),
                  pl.BlockSpec((1, nb, TB, TB * n), lambda g, k: (g + base, last - k, 0, 0)),
                  whole(rate.shape), state, whole(mask.shape), whole((1, width))] + free,
        out_specs=[rows, rows, line, state, pl.BlockSpec((1, TB, width), lambda g, k: (g, 0, 0)), state],
        scratch_shapes=[pltpu.VMEM((n, width), F32), pltpu.VMEM((2, TB * n, width), BF), pltpu.VMEM((2, TB * n, width), BF),
                        pltpu.VMEM((2, TB * n, 128), BF)],
        input_output_aliases=alias, compiler_params=params(), cost_estimate=cost(4), name="backward",
    )(pre, delta, mixed, dy, before, ct, bdiag, rate, qin, mask, skip, *kept)


def conv_back_kernel(dproj_ref, xproj_ref, dmix_ref, inner_ref, prev_ref, rim_ref, taps_ref, shift_ref, carry_ref, *refs,
                     lead, first):
    dinner_ref, tail_ref, head_ref, sums_ref, dm_ref, xs_ref, ds_ref = refs[-7:]
    step, width = dmix_ref.shape[1:]
    k = pl.program_id(1)

    @pl.when(k == 0)
    def _():
        ds_ref[step:] = carry_ref[0]
        sums_ref[0] = jnp.zeros(sums_ref.shape[1:], F32)

    dm_ref[...] = mm(dproj_ref[0], xproj_ref[...])
    xs_ref[:8] = jnp.where(k == pl.num_programs(1) - 1, rim_ref[0], prev_ref[0]) if first else prev_ref[0]
    xs_ref[8:] = inner_ref[0]
    cw = 256

    def tile(x):
        return jnp.sum(x.reshape(step // 8, 8, cw), axis=0)

    for c in range(0, width, cw):
        cs = pl.ds(c, cw)
        pre = shift_ref[:, cs]
        for tap in range(lead + 1):
            pre = pre + taps_ref[tap:tap + 1, cs] * xs_ref[pl.ds(8 - lead + tap, step), cs]
        sig = sigmoid(pre)
        d_conv = (dmix_ref[0, :, cs] + dm_ref[:, cs]) * (sig * (1.0 + pre * (1.0 - sig)))
        ds_ref[:step, cs] = d_conv
        sums_ref[0, :8, cs] += tile(d_conv)
        for tap in range(lead + 1):
            sums_ref[0, 8 + 8 * tap:16 + 8 * tap, cs] += tile(d_conv * xs_ref[pl.ds(8 - lead + tap, step), cs])
        back = taps_ref[lead:lead + 1, cs] * d_conv
        for m in range(1, lead + 1):
            back = back + taps_ref[lead - m:lead - m + 1, cs] * ds_ref[pl.ds(m, step), cs]
        dinner_ref[0, :, cs] = back.astype(BF)

        @pl.when(k == 0)
        def _():
            tail_ref[0, :, cs] = back[step - 8:]

        head_ref[0, :, cs] = d_conv[:8]
        ds_ref[step:, cs] = d_conv[:8]


def conv_back(begin, kept, carry, d_proj, xproj_t, d_mix, inner_x, rim, taps, shift, step=128):
    docs, tokens, width = d_mix.shape
    half = tokens // 2
    last = (begin + half) // step - 1
    count = half // step
    lead = taps.shape[0] - 1
    cols = xproj_t.shape[0]
    rows = pl.BlockSpec((1, step, width), lambda g, k: (g, last - k, 0))
    few = pl.BlockSpec((1, 8, width), lambda g, k: (g, 0, 0))
    sums = 8 * (lead + 2)
    free, alias = chained(kept, 9)
    return pl.pallas_call(
        functools.partial(conv_back_kernel, lead=lead, first=begin == 0),
        out_shape=[shape(d_mix.shape, BF), shape((docs, 8, width)), shape((docs, 8, width)), shape((docs, sums, width))],
        grid=(docs, count),
        in_specs=[pl.BlockSpec((1, step, cols), lambda g, k: (g, count - 1 - k, 0)), whole(xproj_t.shape), rows, rows,
                  pl.BlockSpec((1, 8, width), lambda g, k: (g, jnp.maximum((last - k) * (step // 8) - 1, 0), 0)), few,
                  whole(taps.shape), whole((1, width)), few] + free,
        out_specs=[rows, few, few, pl.BlockSpec((1, sums, width), lambda g, k: (g, 0, 0))],
        scratch_shapes=[pltpu.VMEM((step, width), F32), pltpu.VMEM((step + 8, width), F32), pltpu.VMEM((step + 8, width), F32)],
        input_output_aliases=alias, compiler_params=params(), cost_estimate=cost(0.2), name="conv_back",
    )(d_proj, xproj_t, d_mix, inner_x, inner_x, rim, taps, shift, carry, *kept)


def place_kernel(doc_ref, *refs, pieces):
    parts, (weight_ref, gain_ref, sum_ref) = refs[:pieces], refs[pieces:pieces + 3]
    out_ref, total_ref = refs[-2:]
    j = pl.program_id(0)

    def put(x):
        x = x.astype(F32)
        out_ref[...] = x * gain_ref[...]
        x = x * weight_ref[...].astype(F32)
        x = sum(x[:, c:c + 128] for c in range(0, x.shape[1], 128))
        total_ref[...] = jnp.where(j == 0, sum_ref[...], total_ref[...]) + x

    if pieces == 1:
        put(parts[0][...])
    else:
        for p in range(pieces):
            @pl.when(j == p)
            def _():
                put(parts[p][...])


def place(doc, kept, parts, weight, gain, sums, block, offset):
    rows, width = weight.shape
    docs = width // 2 // block
    at = (lambda j, doc_ref: (0, offset + j)) if len(parts) == 1 else (lambda j, doc_ref: (0, offset + (doc_ref[0] ^ j)))
    one = lambda j, doc_ref: (0, 0)
    piece_at = (lambda j, doc_ref: (0, j)) if len(parts) == 1 else one
    free = [pl.BlockSpec(memory_space=pl.ANY)] * len(kept)
    return pl.pallas_call(
        functools.partial(place_kernel, pieces=len(parts)),
        out_shape=[shape((rows, width)), shape((rows, 128))],
        grid_spec=pltpu.PrefetchScalarGridSpec(
            num_scalar_prefetch=1, grid=(docs,),
            in_specs=[pl.BlockSpec((rows, block), piece_at)] * len(parts)
            + [pl.BlockSpec((rows, block), at), pl.BlockSpec((rows, 1), one), pl.BlockSpec((rows, 128), one)] + free,
            out_specs=[pl.BlockSpec((rows, block), at), pl.BlockSpec((rows, 128), one)]),
        input_output_aliases={4 + len(parts): 0} if kept else {},
        compiler_params=params(), cost_estimate=cost(0.1), name="place",
    )(doc, *parts, weight, gain, sums, *kept)


def input_kernel(part_ref, one_ref, two_ref, hidden_ref, cot_ref, out_ref):
    d_normed = part_ref[...] + one_ref[...].astype(F32) + two_ref[...].astype(F32)
    r = hidden_ref[...].astype(F32)
    scale = lax.rsqrt(jnp.mean(r * r, axis=1, keepdims=True) + NORM_EPS)
    scaled = r * scale
    out_ref[...] = cot_ref[...].astype(F32) + scale * (d_normed - scaled * jnp.mean(d_normed * scaled, axis=1, keepdims=True))


def input_gradient(part, one, two, hidden, cot, step=128):
    rows = pl.BlockSpec((step, hidden.shape[1]), lambda k: (k, 0))
    return pl.pallas_call(
        input_kernel, out_shape=shape(hidden.shape), grid=(hidden.shape[0] // step,),
        in_specs=[rows] * 5, out_specs=rows, compiler_params=params(), cost_estimate=cost(0.1), name="input_gradient",
    )(part, one, two, hidden, cot)


def shifted(block, axis, distance):
    devices = range(lax.axis_size(axis))
    route = [(i - distance, i) for i in devices if i - distance in devices]
    return lax.ppermute(block, axis, route)


def swap(x, axis, flip):
    return lax.ppermute(x, axis, [(i, i ^ flip) for i in range(lax.axis_size(axis))])


def piece(x, index, size, axis):
    return lax.dynamic_slice_in_dim(x, index * size, size, axis)


def chain(decays, states, order, keep, start):
    state = start
    for k in order:
        decay = decays[k].astype(F32)
        state = jnp.where(keep(k), decay * state + states[k].astype(F32), state)
    return state


def doc_gather(x):
    return [x] + [swap(x, "doc", j) for j in (1, 2, 3)]


def doc_sum(parts):
    total = parts[0].astype(F32)
    for j in (1, 2, 3):
        total = total + swap(parts[j].astype(BF), "doc", j).astype(F32)
    return total


def doc_place(parts, doc, axis):
    stack = jnp.stack(parts)
    return jnp.concatenate([lax.dynamic_index_in_dim(stack, doc ^ k, 0, False) for k in range(len(parts))], axis=axis)


def shards(hidden_in, cotangent, scan_init, conv_init, norm_gain, in_weight, conv_weight, conv_bias,
           xproj_weight, dt_weight, dt_bias, a_log, skip_d, out_weight):
    docs, seqs = lax.axis_size("doc"), lax.axis_size("seq")
    doc, seq = lax.axis_index("doc"), lax.axis_index("seq")
    near = seqs == 2 * docs == 8
    hidden, cot = hidden_in[0], cotangent[0]
    tokens, width = hidden.shape
    inner = in_weight.shape[1] // 2
    rank = dt_weight.shape[0]
    states = a_log.shape[0]
    lead = conv_init.shape[1]
    taps = conv_weight.shape[0]
    block = inner // docs
    rows_all = docs * tokens
    blocks = tokens // TB
    middle = tokens // 2
    slots = range(docs)

    def mine(x, offset=0):
        return lax.dynamic_slice_in_dim(x, offset + doc * block, block, x.ndim - 1)

    def mine_of(x, owner):
        return piece(x, owner, block, 1)

    def seq_gather(x):
        return lax.all_gather(x, "seq", axis=0, tiled=True)

    state_rows, lead_rows = states * block // width, 2 * (-(-lead * block // (2 * width)))

    def first_of(j):
        rows = mine_of(conv_init[0], doc ^ j)
        rows = jnp.pad(rows, ((0, lead_rows * width // block - lead), (0, 0))).reshape(lead_rows, width)
        start = mine_of(scan_init[0], doc ^ j).astype(BF).reshape(state_rows, width)
        packed = jnp.concatenate([hidden[tokens - 16:], start, rows], axis=0)
        return jnp.pad(packed, ((0, 32 - packed.shape[0]), (0, 0)))

    halo = [lax.ppermute(first_of(j), ("doc", "seq"),
                         [(d * seqs + s, (d ^ j) * seqs + (s + 1) % seqs) for d in slots for s in range(seqs)])
            for j in slots]
    top, low = hidden[:middle], tie(hidden[middle:], *halo)
    one, two = ([swap(x, "doc", j) for x in (top, low)] for j in (1, 2))
    scaled_weight = (in_weight.astype(F32) * norm_gain.astype(F32)[:, None]).astype(BF)
    w_inner = seq_gather(mine(scaled_weight))
    few = jnp.concatenate([conv_weight, conv_bias[None], dt_bias[None], skip_d[None]], axis=0)
    few = jnp.pad(few, ((0, 16 - few.shape[0]), (0, 0)))
    small = jnp.concatenate([few, a_log, dt_weight, xproj_weight.T], axis=0)
    if near:
        route = [((d, 2 * z + c), (z, 2 * d + c)) for d in slots for z in slots for c in range(2)]
        turn = [(a * seqs + b, e * seqs + f) for (a, b), (e, f) in route]
        half = lax.ppermute(small, ("doc", "seq"), turn)
        half = tie(half, *one, *two)
        other = swap(half, "seq", 1)
        core = seq % 2 == 0
        small = jnp.concatenate([jnp.where(core, half, other), jnp.where(core, other, half)], axis=1)
    else:
        small = mine(lax.all_gather(small, "seq", axis=1, tiled=True))
    three = [swap(two[0], "doc", 1), swap(one[1], "doc", 2)]
    w_gate = seq_gather(tie(mine(scaled_weight, inner), small))
    w_out = seq_gather(mine(out_weight))

    wide = small.astype(F32)
    conv_taps, conv_shift, dt_shift, skip = wide[:taps], wide[taps][None], wide[taps + 1][None], wide[taps + 2][None]
    at = 16
    rate = -jnp.exp(wide[at:at + states])
    dt_full = small[at + states:at + states + rank]
    xproj_t = small[at + states + rank:]
    rate2 = rate * (1.0 / LN2)

    is_first = (seq == 0).astype(jnp.int32)[None]

    def first_rows(x):
        rows = x[16 + state_rows:16 + state_rows + lead_rows].reshape(-1, block)[:lead].astype(F32)
        return jnp.pad(rows, ((8 - lead, 0), (0, 0)))

    kept, proj_part = (), []
    for j, x in enumerate(((top, low), one, two, three)):
        if j == 3:
            x = [tie(half, kept[0]) for half in three]
            cot_top = tie(cot[:middle], *x)
            cot_near = [swap(cot_top, "doc", 1), swap(cot_top, "doc", 2)]
        *kept, part = front(j, docs, kept, is_first, *x, halo[j], w_inner, small, lead,
                            rank + 2 * states, first_rows(halo[j]))
        proj_part.append(part)
    normed, inner_x, mixed, rim = kept
    mixed_flat = mixed.reshape(rows_all, block)

    w_gate = tie(w_gate, *proj_part)
    gate_in = mm(normed, w_gate)
    got = [tie(swap(proj_part[j].astype(BF), "doc", j), gate_in) for j in slots[1:]]
    proj_own = (proj_part[0] + sum(x.astype(F32) for x in got)).astype(BF)
    proj = jnp.concatenate(doc_gather(proj_own), axis=0)
    proj = tie(proj, *cot_near)
    cot_low = tie(cot[middle:], proj)
    cot_rest = [swap(cot_low, "doc", 1), swap(cot_low, "doc", 2)]
    cot_far = [swap(tie(cot_near[1], proj), "doc", 1)]
    init = jnp.stack([x[16:16 + state_rows].reshape(states, block) for x in halo]).astype(F32)
    rank_in = proj[:, :rank]
    gate_in = gate_in.reshape(docs, tokens, block)

    mask = jnp.repeat(jnp.eye(TB, dtype=F32), states, axis=1)
    spread = jnp.tile(jnp.eye(states, dtype=BF), (1, TB))

    def columns(x):
        return jnp.swapaxes(x.reshape(docs, blocks, TB, states), 2, 3).astype(F32)

    def diagonal(x):
        return (mm(x, spread).reshape(docs, blocks, TB, TB * states) * mask).astype(BF)

    b_rows, c_rows = proj[:, rank:rank + states], proj[:, rank + states:]
    b_cols, c_cols = columns(b_rows), columns(c_rows)
    b_diag, c_diag = diagonal(b_rows), diagonal(c_rows)

    rank_in = rank_in.reshape(docs, tokens, rank)
    part = docs // 2
    starts, decays = {}, {}
    kept = ()
    for base in (part, 0):
        *kept, end_state, decay = summary(base, part, kept, rank_in, dt_full, dt_shift, mixed, b_cols, rate2)
        if base == 0:
            end_state = tie(end_state, *cot_far)
        ends = lax.all_gather(jnp.stack([end_state, decay]).astype(BF), "seq")
        decays[base] = ends[:, 1]
        starts[base] = chain(ends[:, 1], ends[:, 0], range(seqs), lambda k: k < seq, init[base:base + part])
        if base:
            cot_far.append(swap(tie(cot_rest[0], end_state), "doc", 2))
            kept[0] = tie(kept[0], cot_rest[0], w_out)
    dt_pre, delta = kept
    rank_in = rank_in.reshape(rows_all, rank)

    cot_all = jnp.concatenate([cot_top, cot_low, cot_near[0], cot_rest[0], cot_near[1], cot_rest[1], *cot_far], axis=0)
    cot_all = tie(cot_all, end_state)
    def relay_far(x):
        x, half = x.astype(BF), x.shape[0] // 32 * 16
        return swap(x[:half], "doc", 1), swap(x[half:], "doc", 2)

    def relay_near(parts, one, two):
        half = one.shape[0]
        first = jnp.concatenate([parts[1][:half], parts[1][half:] + two.astype(F32)], axis=0).astype(BF)
        second = jnp.concatenate([parts[2][:half] + one.astype(F32), parts[2][half:]], axis=0).astype(BF)
        return first, second

    d_start, skip_grad, out_rows = {}, [], {}
    kept = ()
    for base in (part, 0):
        rows = slice(base * tokens, (base + part) * tokens)
        d_gated = mm(cot_all[rows], w_out).reshape(part, tokens, block)
        if base == 0:
            d_gated = tie(d_gated, *out_rows.values())
        *kept, d_start[base], skip_part = forward(base, part, kept, delta, mixed, gate_in, d_gated, b_cols, c_diag, rate2,
                                                  starts[base], mask, skip)
        skip_grad.append(skip_part)
        for j in range(base + part - 1, base - 1, -1):
            out_rows[j] = mm_last(kept[2][j], w_out)
        if base:
            out_far = relay_far(out_rows[3])
    out_far = [tie(x, d_start[0]) for x in out_far]
    d_y, before, gated, d_gate, d_out = kept
    gated, d_gate = gated.reshape(rows_all, block), d_gate.reshape(rows_all, block)
    skip_grad = sum(jnp.sum(x, axis=(0, 1)) for x in skip_grad)
    later = lax.all_gather(jnp.concatenate([d_start[0], d_start[part]], axis=0).astype(BF), "seq")
    decays = jnp.concatenate([decays[0], decays[part]], axis=1)
    zero = jnp.zeros((docs, states, block), F32)
    back = range(seqs - 1, -1, -1)
    later_sum = chain(decays, later, back, lambda k: k > seq, zero)
    first_sum = chain(decays, later, back, lambda k: True, zero)

    def seq_sum(x):
        return lax.psum_scatter(x, "seq", scatter_dimension=0, tiled=True)

    def all_blocks(total):
        return lax.all_gather(total, "doc", axis=1, tiled=True)

    out_first, out_second = relay_near(out_rows, *out_far)
    out_got = swap(out_first, "doc", 1), swap(out_second, "doc", 2)
    gated = tie(gated, out_first, out_second)
    out_part = mm_first(cot_all, gated).astype(BF)
    gate_part = mm_first(normed, d_gate).astype(BF)
    later_sum = tie(later_sum, out_part, gate_part)
    out_part, gate_part = seq_sum(out_part), seq_sum(gate_part)

    d_out = d_out.reshape(docs, tokens, states)

    def proj_parts(kept, begin):
        rows = slice(begin, begin + middle)
        d_rank = mm_last(kept[0][:, rows].reshape(docs * middle, block), dt_full).reshape(docs, middle, rank)
        d_in = kept[2].reshape(docs, tokens, states)[:, rows]
        full = jnp.concatenate([d_rank, d_in, d_out[:, rows]], axis=2)
        return full[0], [full[j].astype(BF) for j in slots[1:]]

    def run_back(begin, kept, state):
        return backward(0, docs, begin, kept, dt_pre, delta, mixed, d_y, before, c_cols, b_diag, rate2, state, mask, skip)

    *kept, rate_grad, dt_bias_grad, passed_on = run_back(middle, (), later_sum)
    kept[0] = tie(kept[0], *out_got)
    out_got = [tie(x, kept[2]) for x in out_got]
    out_total = all_blocks(tie(out_part, kept[2]))
    own_late, sent = proj_parts(kept, middle)
    got = [swap(x, "doc", j) for j, x in zip(slots[1:], sent)]
    kept[0] = tie(kept[0], *sent)
    *kept, rate_part, bias_part, _ = run_back(0, kept, passed_on)
    got = [tie(x, kept[2]) for x in got]
    own_late = (own_late + sum(x.astype(F32) for x in got)).astype(BF)
    kept[0] = tie(kept[0], own_late, out_total)
    gate_total = all_blocks(tie(gate_part, kept[2]))
    late = [own_late] + [swap(own_late, "doc", j) for j in slots[1:]]
    d_pre, d_mix, _ = kept
    rate_grad = jnp.sum(rate_grad + rate_part, axis=0)
    dt_bias_grad = jnp.sum(dt_bias_grad + bias_part, axis=(0, 1))
    own_early, sent = proj_parts(kept, 0)
    got = [swap(x, "doc", j) for j, x in zip(slots[1:], sent)]

    nothing = jnp.zeros((docs, 8, block), F32)
    d_proj_late = tie(jnp.stack(late), *sent)
    d_inner, tail, carry, sums_late = conv_back(middle, (), nothing, d_proj_late, xproj_t, d_mix, inner_x, rim, conv_taps,
                                                conv_shift)
    d_gate = tie(d_gate, *sent).reshape(docs, tokens, block)
    gate_far = mm_last(d_gate[3], w_gate)
    own_early = (own_early + sum(x.astype(F32) for x in got)).astype(BF)
    d_inner = tie(d_inner, own_early)
    early = [own_early] + [swap(own_early, "doc", j) for j in slots[1:]]

    d_inner = tie(d_inner, gate_far, *early[1:])
    d_proj_early = jnp.stack(early)
    d_proj = jnp.concatenate([d_proj_early, d_proj_late], axis=1).reshape(rows_all, -1)
    few = jnp.concatenate([rate_grad, dt_bias_grad[None], skip_grad[None], jnp.zeros((14, block), F32)], axis=0)
    small_grad = [few, mm_first(rank_in, d_pre.reshape(rows_all, block)),
                  mm_first(d_proj, mixed_flat)]
    if near:
        side = seq % 2
        small_sum, sent = (jnp.concatenate([piece(x, at_side, block // 2, 1) for x in small_grad], axis=0)
                           for at_side in (side, 1 - side))
        small_sum = (small_sum + swap(sent.astype(BF), "seq", 1).astype(F32)).astype(BF)
        turned = lax.ppermute(small_sum, ("doc", "seq"), turn)
        d_proj_early = tie(d_proj_early, small_sum, gate_total)
    else:
        small_grad = jnp.concatenate(small_grad, axis=0)
        small_sum = lax.psum_scatter(small_grad, "seq", scatter_dimension=1, tiled=True)
        small_sum = lax.all_gather(small_sum.astype(BF), ("doc", "seq"), axis=1, tiled=True)
        turned = piece(small_sum, seq, inner // seqs, 1).astype(F32)

    d_inner, _, head, sums = conv_back(0, [d_inner], carry, d_proj_early, xproj_t, d_mix, inner_x, rim, conv_taps, conv_shift)
    d_ext = jnp.stack([sum(conv_taps[k] * head[:, j - k] for k in range(j + 1)) for j in range(lead)], axis=1)
    passed = shifted(d_ext.astype(BF), "seq", -1).astype(F32)
    d_inner = lax.dynamic_update_slice(d_inner, (tail[:, 8 - lead:] + passed).astype(BF), (0, tokens - lead, 0))
    d_inner = tie(d_inner, turned)
    inner_part = mm_first(normed, d_inner.reshape(rows_all, block)).astype(BF)
    d_inner = tie(d_inner, inner_part)
    inner_part = seq_sum(inner_part)
    small_sum = sum(x.astype(F32) for x in doc_gather(turned)) if near else turned
    d_inner = tie(d_inner, small_sum)

    d_gate = tie(d_gate, d_inner)

    def normed_part(j):
        return mm_last(d_inner[j], w_inner) + mm_last(d_gate[j], w_gate)

    far = mm_last(d_inner[3], w_inner) + gate_far
    far_got = relay_far(far)
    d_inner = tie(d_inner, far)
    parts = [normed_part(j) for j in range(3)]
    first, second = relay_near(parts, *(tie(x, parts[0]) for x in far_got))
    early_got = swap(first, "doc", 1), swap(second, "doc", 2)
    inner_total = all_blocks(tie(inner_part, first, second))
    gain = norm_gain.astype(F32)[:, None]
    in_total, gain_sum = place(doc[None], [], [gate_total], in_weight, gain, jnp.zeros((width // seqs, 128), F32), block, docs)

    output = (hidden.astype(F32) + out_rows[0] + sum(x.astype(F32) for x in out_got)).astype(BF)
    sums = jnp.sum((sums + sums_late).reshape(docs, taps + 1, 8, block), axis=(0, 2))
    ends = jnp.concatenate([jnp.where(seq == 0, tie(d_ext, *early_got, inner_part), 0.0).reshape(docs * lead, block), sums], axis=0)
    if near:
        for flip in (1, 2, 4):
            ends = ends + swap(ends, "seq", flip)
    else:
        ends = lax.psum(ends, "seq")
    sends = [jnp.concatenate([first_sum[j], ends[j * lead:(j + 1) * lead], ends[docs * lead:]], axis=0) for j in slots]
    ends = doc_place([sends[0]] + [swap(sends[j], "doc", j) for j in slots[1:]], doc, 1)
    init_grad, conv_sum = ends[:states + lead], piece(ends[states + lead:], seq, inner // seqs, 1)
    input_grad = input_gradient(parts[0], *early_got, hidden, cot)
    in_total, gain_sum = place(doc[None], [in_total], [inner_total], in_weight, gain, gain_sum, block, 0)
    gain_sum = jnp.sum(gain_sum, axis=1)

    return (
        output[None],
        input_grad[None],
        init_grad[None, :states],
        init_grad[None, states:],
        gain_sum,
        in_total,
        conv_sum[1:],
        conv_sum[0],
        small_sum[states + 16 + rank:].T,
        small_sum[states + 16:states + 16 + rank],
        small_sum[states],
        small_sum[:states],
        small_sum[states + 1],
        out_total.astype(F32),
    )


def solution(mesh):
    placed = (
        P("doc", "seq", None), P("doc", "seq", None), P("doc", None, None), P("doc", None, None),
        P("seq"), P("seq", None), P(None, "seq"), P("seq"), P("seq", None), P(None, "seq"),
        P("seq"), P(None, "seq"), P("seq"), P("seq", None),
    )
    return jax.shard_map(shards, mesh=mesh, in_specs=placed, out_specs=placed, check_vma=False)
```
